32 devices in a mesh: outer: 4 (over z), inner: 8 (over y, x, core).
Axes of the slice: x: 2, y: 2, z: 4, core: 2. Of those that a mesh axis runs over, the one named last changes fastest.
Arguments:
- tiles: bfloat16 [4096, 128, 128], P(('outer', 'inner')), as said below
- tile_row: int32 [4096], P(('outer', 'inner')), may hold values from 0 to 3, as said below
- tile_col: int32 [4096], P(('outer', 'inner')), may hold values from 0 to 3, as said below
- counts: int32 [1024], P(('outer', 'inner')), may hold values from 1 to 4, as said below
- vectors: bfloat16 [16384, 64], P(('outer', 'inner')), may hold values from -6 to 6
Outputs:
- basis: float32 [16384, 64], P(('outer', 'inner'))
- degree: float32 [16384], P(('outer', 'inner'))
The draws below stay inside these ranges and needn't reach their ends.
Inputs may be any that keep to these rules, and one draw needn't show every extreme that they name: Slot s from sender g to destination h is live exactly when s < counts[g * 32 + h]; the tiles of dead slots hold values that are no part of P. counts is 4 from every sender to itself and 1 to 4 from every sender to every other destination. `tile_row`: A slot from a sender to itself with number s lies in block row s % 4. `tile_col`: A slot from a sender to itself with number s lies in block column s % 4. `tiles`: entries are affinities, zero or positive.
All inputs are finite; a program needn't handle non-finite values.
Results may differ from the reference program's by a relative error of at most 0.004.
Values may be sent and summed in bfloat16 or wider, within the bound.
A program may use at most 192 MiB of HBM per device.

```python
import math
import jax
import jax.numpy as jnp
from jax import lax

TILE_SIDE = 128
K = 64
SLOTS = 4
DEVICE_ROW_BLOCKS = 4
PEERS = 32
POINTS = 16384
TILE_SLOT_TOTAL = 4096


def draw_tiles(key, part):
    key_value, key_degree_scale = jax.random.split(key, 2)
    array_extent = (TILE_SLOT_TOTAL, TILE_SIDE, TILE_SIDE)
    spread = jax.random.uniform(key_value, array_extent, dtype=jnp.float32)
    row_degree_scale = jnp.exp(jax.random.uniform(key_degree_scale, (TILE_SLOT_TOTAL, TILE_SIDE, 1), dtype=jnp.float32, minval=0.0, maxval=math.log(10.0)))
    values = 3.2 * jnp.exp(-16.0 * spread)
    return (values * row_degree_scale / TILE_SIDE).astype(jnp.bfloat16)


def slot_layout():
    slot_numbers_list = jnp.arange(TILE_SLOT_TOTAL, dtype=jnp.int32)
    sender = slot_numbers_list // (PEERS * SLOTS)
    target = slot_numbers_list // SLOTS % PEERS
    number = slot_numbers_list % SLOTS
    return (sender, target, number)


def draw_tile_row(key, part):
    sender, target, number = slot_layout()
    selected_entries = jax.random.randint(jax.random.fold_in(key, 11), (TILE_SLOT_TOTAL,), 0, DEVICE_ROW_BLOCKS, dtype=jnp.int32)
    return jnp.where(sender == target, number % DEVICE_ROW_BLOCKS, selected_entries).astype(jnp.int32)


def draw_tile_col(key, part):
    sender, target, number = slot_layout()
    selected_entries = jax.random.randint(jax.random.fold_in(key, 12), (TILE_SLOT_TOTAL,), 0, DEVICE_ROW_BLOCKS, dtype=jnp.int32)
    return jnp.where(sender == target, number % DEVICE_ROW_BLOCKS, selected_entries).astype(jnp.int32)


def draw_counts(key, part):
    pair_ids = jnp.arange(PEERS * PEERS, dtype=jnp.int32)
    sender = pair_ids // PEERS
    target = pair_ids % PEERS
    chosen = jax.random.randint(jax.random.fold_in(key, 21), (PEERS * PEERS,), 1, SLOTS + 1, dtype=jnp.int32)
    return jnp.where(sender == target, SLOTS, chosen).astype(jnp.int32)


def block_scale(key, shape, pieces, smallest, high):
    def one(dim, shards_of):
        draws = jax.random.uniform(jax.random.fold_in(jax.random.fold_in(key, 6), dim), (shards_of,), jnp.float32, smallest / len(pieces), high / len(pieces))
        return jnp.repeat(jnp.exp(draws), shape[dim] // shards_of).reshape((-1,) + (1,) * (len(shape) - dim - 1))

    level = one(*pieces[0])
    for cut in pieces[1:]:
        level = level * one(*cut)
    return level


def noise(key, extent, deviation, limit, cuts=(), kind=jnp.bfloat16):
    gain = block_scale(key, extent, cuts, -0.22, 0.18) if cuts else 1.0
    array = jax.random.normal(key, extent, jnp.float32) * deviation * gain
    return jnp.minimum(jnp.maximum(array, -limit), limit).astype(kind)


def setup_inputs(seed: int = 0) -> dict:
    key_list = jax.random.split(jax.random.key(seed), 6)
    tiles = draw_tiles(jax.random.fold_in(key_list[5], 71), 0)
    tile_row = draw_tile_row(jax.random.fold_in(key_list[5], 71), 0)
    tile_col = draw_tile_col(jax.random.fold_in(key_list[5], 71), 0)
    counts = draw_counts(jax.random.fold_in(key_list[5], 71), 0)
    vectors = noise(key_list[4], (POINTS, K), 1.0, 6.0, ((0, 32),))
    return {"tiles": tiles, "tile_row": tile_row, "tile_col": tile_col, "counts": counts, "vectors": vectors}


def reference(tiles, tile_row, tile_col, counts, vectors):
    slot_numbers_list = jnp.arange(TILE_SLOT_TOTAL, dtype=jnp.int32)
    sender = slot_numbers_list // (PEERS * SLOTS)
    target = slot_numbers_list // SLOTS % PEERS
    number = slot_numbers_list % SLOTS
    live = (number < counts[sender * PEERS + target]).astype(jnp.float32)
    row_block = (sender * DEVICE_ROW_BLOCKS + tile_row).astype(jnp.int32)
    col_block = (target * DEVICE_ROW_BLOCKS + tile_col).astype(jnp.int32)
    row_sums = lax.optimization_barrier(jnp.sum(tiles.astype(jnp.float32), axis=2)) * live[:, None]
    col_sums = lax.optimization_barrier(jnp.sum(tiles.astype(jnp.float32), axis=1)) * live[:, None]
    degree_blocks = jnp.zeros((PEERS * DEVICE_ROW_BLOCKS, TILE_SIDE), jnp.float32)
    degree_blocks = degree_blocks.at[row_block].add(row_sums).at[col_block].add(col_sums)
    degree = 1.0 + degree_blocks.reshape(POINTS)
    inv_root = lax.rsqrt(degree)
    scaled = (inv_root[:, None] * vectors.astype(jnp.float32)).astype(jnp.bfloat16)
    scaled_blocks = scaled.astype(jnp.float32).reshape(PEERS * DEVICE_ROW_BLOCKS, TILE_SIDE, K)
    group_tiles = tiles.reshape(PEERS, PEERS * SLOTS, TILE_SIDE, TILE_SIDE)
    group_rows = row_block.reshape(PEERS, PEERS * SLOTS)
    group_cols = col_block.reshape(PEERS, PEERS * SLOTS)
    group_live = live.reshape(PEERS, PEERS * SLOTS)

    def step(total, inputs):
        block_tiles, rows_here, cols_here, live_here = inputs
        dense = block_tiles.astype(jnp.float32)
        forward = jnp.einsum('tab,tbk->tak', dense, scaled_blocks[cols_here])
        mirrored = jnp.einsum('tba,tbk->tak', dense, scaled_blocks[rows_here])
        mirrored = lax.optimization_barrier(mirrored.astype(jnp.bfloat16)).astype(jnp.float32)
        total = total.at[rows_here].add(forward * live_here[:, None, None])
        total = total.at[cols_here].add(mirrored * live_here[:, None, None])
        return (total, None)
    start = jnp.zeros((PEERS * DEVICE_ROW_BLOCKS, TILE_SIDE, K), jnp.float32)
    total, _ = lax.scan(step, start, (group_tiles, group_rows, group_cols, group_live))
    image = inv_root[:, None] * (total.reshape(POINTS, K) + scaled.astype(jnp.float32))
    gram = jnp.dot(image.T, image, precision=lax.Precision.HIGHEST) / jnp.float32(POINTS)
    lower = jnp.linalg.cholesky(gram)
    basis = jax.scipy.linalg.solve_triangular(lower, image.T, lower=True).T
    return (basis, degree)
```

```python
import functools

import jax
import jax.numpy as jnp
from jax import lax
from jax.experimental import pallas as pl
from jax.experimental.pallas import tpu as pltpu
from jax.sharding import PartitionSpec as P

MESH = pl.DeviceIdType.MESH
BF = jnp.bfloat16
F32 = jnp.float32
NT = (((1,), (1,)), ((), ()))
HI = lax.Precision.HIGHEST


def exchange(
    no, ni, ns, nb, k, ts,
    row_ref, col_ref, cnt_ref, tiles_hbm, v_ref,
    img_ref, deg_ref, gram_ref,
    tiles, vall, csum, crecv, invall, own, mout, rcore, asum, rplane, bsum, rz, fwd, ginner, gz,
    tile_sem, vz_s, vz_r, vp_s, vp_r, vc_s, vc_r, cs_s, cs_r, iv_s, iv_r,
    rc_s, rc_r, rp_s, rp_r, rz_s, rz_r, g1_s, g1_r, g2_s, g2_r,
):
    nc = ni // 2
    n = no * ni
    z = lax.axis_index("outer")
    i = lax.axis_index("inner")
    me = z * ni + i
    chip = i // 2
    core = i % 2
    sib = chip * 2 + (1 - core)

    def zof(d):
        return lax.rem(z + d, no)

    def cof(d):
        return lax.rem(chip + d, nc)

    def iof(d):
        return lax.rem(i + d, ni)

    def hof(d):
        return lax.rem(me + d, n)

    def loop(lo, hi, body):
        def step(j, carry):
            body(j)
            return carry
        lax.fori_loop(lo, hi, step, 0)

    def remote(src, dst, ssem, rsem, zz, ii):
        return pltpu.make_async_remote_copy(
            src_ref=src, dst_ref=dst, send_sem=ssem, recv_sem=rsem,
            device_id=(zz, ii), device_id_type=MESH)

    def tile_copy(q):
        part = pl.ds(q * ni, ni)
        return pltpu.make_async_copy(tiles_hbm.at[part], tiles.at[part], tile_sem.at[q])

    for q in range(no):
        tile_copy(q).start()

    barrier = pltpu.get_barrier_semaphore()

    def greet(d):
        h = hof(d)
        pl.semaphore_signal(barrier, inc=1, device_id=(h // ni, h % ni), device_id_type=MESH)
    loop(1, n, greet)
    pl.semaphore_wait(barrier, n - 1)

    def vz(d):
        return remote(v_ref, vall.at[me], vz_s.at[d], vz_r.at[z], zof(d), i)

    def vz_in(d):
        zz = zof(d)
        return remote(v_ref, vall.at[zz * ni + i], vz_s.at[d], vz_r.at[zz], zz, i)

    def vp(zd, d):
        zz = zof(zd)
        slot = vall.at[zz * ni + i]
        return remote(slot, slot, vp_s.at[zd, d], vp_r.at[zz, chip], z, cof(d) * 2 + core)

    def vp_in(zd, d):
        zz, cc = zof(zd), cof(d)
        slot = vall.at[zz * ni + cc * 2 + core]
        return remote(slot, slot, vp_s.at[zd, d], vp_r.at[zz, cc], z, cc * 2 + core)

    def vc(zd, d):
        zz, cc = zof(zd), cof(d)
        slot = vall.at[zz * ni + cc * 2 + core]
        return remote(slot, slot, vc_s.at[zd, d], vc_r.at[zz, cc], z, sib)

    def vc_in(zd, d):
        zz, cc = zof(zd), cof(d)
        slot = vall.at[zz * ni + cc * 2 + (1 - core)]
        return remote(slot, slot, vc_s.at[zd, d], vc_r.at[zz, cc], z, sib)

    vall[me] = v_ref[...]
    loop(1, no, lambda d: vz(d).start())
    loop(1, nc, lambda d: vp(0, d).start())
    vc(0, 0).start()

    iota8 = lax.broadcasted_iota(jnp.int32, (8, ts), 0)

    def live_index(ref, h, s):
        return jnp.where(s < cnt_ref[h], ref[h * ns + s], -1)

    def sums(h, racc):
        t = tiles[h]
        wc = jnp.concatenate(
            [jnp.where(iota8 == live_index(col_ref, h, s), 1.0, 0.0).astype(BF) for s in range(ns)], axis=1)
        csum[h] = jnp.dot(wc, t, preferred_element_type=F32)[:nb]
        for s in range(ns):
            wr = jnp.where(iota8 == live_index(row_ref, h, s), 1.0, 0.0).astype(BF)
            racc = racc + lax.dot_general(wr, t[s * ts:(s + 1) * ts], NT, preferred_element_type=F32)
        return racc

    racc = jnp.zeros((8, ts), F32)
    for q in range(no):
        tile_copy(q).wait()
        racc = lax.fori_loop(q * ni, (q + 1) * ni, sums, racc)

    def cs(d):
        h = hof(d)
        return remote(csum.at[h], crecv.at[me], cs_s.at[d], cs_r.at[me], h // ni, h % ni)

    def cs_in(d):
        h = hof(d)
        return remote(csum.at[h], crecv.at[h], cs_s.at[d], cs_r.at[h], h // ni, h % ni)

    loop(1, n, lambda d: cs(d).start())

    def relay_z(zd):
        vz_in(zd).wait_recv()
        loop(1, nc, lambda d: vp(zd, d).start())
        vc(zd, 0).start()
    loop(1, no, relay_z)

    def add_sums(d, acc):
        cs_in(d).wait_recv()
        return acc + crecv[hof(d)]
    degree = lax.fori_loop(1, n, add_sums, 1.0 + racc[:nb] + csum[me])
    deg_ref[...] = degree
    invall[me] = lax.rsqrt(degree)

    def iv(d):
        h = hof(d)
        return remote(invall.at[me], invall.at[me], iv_s.at[d], iv_r.at[me], h // ni, h % ni)

    def iv_in(d):
        h = hof(d)
        return remote(invall.at[h], invall.at[h], iv_s.at[d], iv_r.at[h], h // ni, h % ni)

    loop(1, n, lambda d: iv(d).start())

    inv = invall[me]
    for b in range(nb):
        own[b] = (inv[b:b + 1] * v_ref[b].astype(F32)).astype(BF).astype(F32)

    def mirror(zz, cc, half):
        h = zz * ni + cc * 2 + half
        parts = [[] for _ in range(nb)]
        for s in range(ns):
            c = live_index(col_ref, h, s)
            rows = own[row_ref[h * ns + s]]
            for b in range(nb):
                parts[b].append((rows * jnp.where(c == b, 1.0, 0.0)).astype(BF))
        left = jnp.concatenate([jnp.concatenate(p, axis=1) for p in parts], axis=0)
        m = jnp.dot(left, tiles[h], preferred_element_type=F32)
        mout[half, zz, cc] = m.astype(BF).reshape(nb, k, ts)

    def rc(zd):
        zz = zof(zd)
        return remote(mout.at[1 - core, zz], rcore.at[zz], rc_s.at[zz], rc_r.at[zz], z, sib)

    def rp(zd, d):
        zz, cc = zof(zd), cof(d)
        return remote(asum.at[zz, cc], rplane.at[zz, chip], rp_s.at[zd, d], rp_r.at[zz, chip], z, cc * 2 + core)

    def rp_in(zd, d):
        zz, cc = zof(zd), cof(d)
        return remote(asum.at[zz, cc], rplane.at[zz, cc], rp_s.at[zd, d], rp_r.at[zz, cc], z, cc * 2 + core)

    def rzc(zd):
        return remote(bsum.at[zof(zd)], rz.at[z], rz_s.at[zd], rz_r.at[z], zof(zd), i)

    def rz_in(zd):
        zz = zof(zd)
        return remote(bsum.at[zz], rz.at[zz], rz_s.at[zd], rz_r.at[zz], zz, i)

    def make_chunk(zo):
        zd = lax.rem(zo + 1, no)
        zz = zof(zd)
        loop(0, nc, lambda cc: mirror(zz, cc, 1 - core))
        rc(zd).start()
        loop(0, nc, lambda cc: mirror(zz, cc, core))
    loop(0, no, make_chunk)

    def send_chunk(zo):
        zd = lax.rem(zo + 1, no)
        zz = zof(zd)
        rc(zd).wait_recv()

        def add_one(d):
            cc = cof(d)
            asum[zz, cc] = (mout[core, zz, cc].astype(F32) + rcore[zz, cc].astype(F32)).astype(BF)

        def add_send(d):
            add_one(d)
            rp(zd, d).start()
        loop(1, nc, add_send)
        add_one(0)
    loop(0, no, send_chunk)

    def relay_p(zd):
        def one(d):
            vp_in(zd, d).wait_recv()
            vc(zd, d).start()
        loop(1, nc, one)
    loop(0, no, relay_p)
    loop(1, n, lambda d: iv_in(d).wait_recv())
    loop(0, no, lambda zd: loop(0, nc, lambda d: vc_in(zd, d).wait_recv()))

    fwd[...] = jnp.zeros_like(fwd)

    def forward(h):
        acc = fwd[...]
        for s in range(ns):
            c = col_ref[h * ns + s]
            r = live_index(row_ref, h, s)
            blk = (inv_row(h, c) * vall[h, c].astype(F32)).astype(BF).astype(F32)
            left = jnp.concatenate([(blk * jnp.where(r == b, 1.0, 0.0)).astype(BF) for b in range(nb)], axis=0)
            acc = acc + lax.dot_general(left, tiles[h, s * ts:(s + 1) * ts], NT, preferred_element_type=F32)
        fwd[...] = acc

    def inv_row(h, c):
        rows = invall[h]
        out = rows[0:1]
        for b in range(1, nb):
            out = jnp.where(jnp.broadcast_to(c, out.shape) == b, rows[b:b + 1], out)
        return out

    def work(zo):
        zd = lax.rem(zo + 1, no)
        zz = zof(zd)
        loop(zz * ni, (zz + 1) * ni, forward)
        total = asum[zz, chip].astype(F32)

        def add_p(d, acc):
            rp_in(zd, d).wait_recv()
            return acc + rplane[zz, cof(d)].astype(F32)
        total = lax.fori_loop(1, nc, add_p, total)
        bsum[zz] = total.astype(BF)

    def work_send(zo):
        work(zo)
        rzc(lax.rem(zo + 1, no)).start()
    loop(0, no - 1, work_send)
    work(no - 1)

    def add_z(d, acc):
        rz_in(d).wait_recv()
        return acc + rz[zof(d)].astype(F32)
    total = lax.fori_loop(1, no, add_z, bsum[z].astype(F32))
    gram = jnp.zeros((k, k), F32)
    for b in range(nb):
        x = inv[b:b + 1] * (total[b] + fwd[b * k:(b + 1) * k] + own[b])
        img_ref[b] = x
        gram = gram + lax.dot_general(x, x, NT, preferred_element_type=F32, precision=HI)
    half = k // 2
    ginner[i] = jnp.concatenate([gram[:half], gram[half:]], axis=1)

    def g1(d):
        return remote(ginner.at[i], ginner.at[i], g1_s.at[d], g1_r.at[i], z, iof(d))

    def g1_in(d):
        ii = iof(d)
        return remote(ginner.at[ii], ginner.at[ii], g1_s.at[d], g1_r.at[ii], z, ii)

    def g2(d):
        return remote(gz.at[z], gz.at[z], g2_s.at[d], g2_r.at[z], zof(d), i)

    def g2_in(d):
        zz = zof(d)
        return remote(gz.at[zz], gz.at[zz], g2_s.at[d], g2_r.at[zz], zz, i)

    loop(1, ni, lambda d: g1(d).start())
    loop(1, ni, lambda d: g1_in(d).wait_recv())
    gz[z] = lax.fori_loop(1, ni, lambda j, a: a + ginner[j], ginner[0])
    loop(1, no, lambda d: g2(d).start())
    loop(1, no, lambda d: g2_in(d).wait_recv())
    g = lax.fori_loop(1, no, lambda j, a: a + gz[j], gz[0])
    gram_ref[...] = g * (1.0 / (n * nb * ts))

    loop(1, no, lambda d: vz(d).wait_send())
    loop(0, no, lambda zd: loop(1, nc, lambda d: vp(zd, d).wait_send()))
    loop(0, no, lambda zd: loop(0, nc, lambda d: vc(zd, d).wait_send()))
    loop(1, n, lambda d: cs(d).wait_send())
    loop(1, n, lambda d: iv(d).wait_send())
    loop(0, no, lambda zd: rc(zd).wait_send())
    loop(0, no, lambda zd: loop(1, nc, lambda d: rp(zd, d).wait_send()))
    loop(1, no, lambda zd: rzc(zd).wait_send())
    loop(1, ni, lambda d: g1(d).wait_send())
    loop(1, no, lambda d: g2(d).wait_send())


def orthonormalize(k, gram_ref, img_ref, out_ref):
    g = gram_ref[...]
    a = jnp.concatenate([g[:, :k], g[:, k:]], axis=0)
    row = lax.broadcasted_iota(jnp.int32, (k, k), 0)
    col = lax.broadcasted_iota(jnp.int32, (k, k), 1)
    a = jnp.concatenate([a, jnp.where(row == col, 1.0, 0.0)], axis=1)
    rows = lax.broadcasted_iota(jnp.int32, (k, 2 * k), 0)
    scale = jnp.zeros((k, 2 * k), F32)
    for j in range(k):
        c = jnp.broadcast_to(a[:, j:j + 1], (k, 2 * k))
        piv = c[j:j + 1]
        scale = jnp.where(rows == j, c, scale)
        a = a - jnp.where(rows > j, c, 0.0) * (a[j:j + 1] / piv)
    inv_low = (a * lax.rsqrt(scale))[:, k:]
    for b in range(img_ref.shape[0]):
        ts = img_ref.shape[2]
        out_ref[b * ts:(b + 1) * ts, :] = lax.dot_general(
            img_ref[b], inv_low, (((0,), (1,)), ((), ())), preferred_element_type=F32, precision=HI)


def shards(tiles, tile_row, tile_col, counts, vectors):
    no, ni = lax.axis_size("outer"), lax.axis_size("inner")
    n = no * ni
    nc = ni // 2
    ns = tiles.shape[0] // n
    ts = tiles.shape[1]
    k = vectors.shape[1]
    nb = vectors.shape[0] // ts
    vt = jnp.swapaxes(vectors.reshape(nb, ts, k), 1, 2)
    dma = pltpu.SemaphoreType.DMA
    blk = (nb, k, ts)
    vmem = pl.BlockSpec(memory_space=pltpu.VMEM)
    smem = pl.BlockSpec(memory_space=pltpu.SMEM)
    img, deg, gram = pl.pallas_call(
        functools.partial(exchange, no, ni, ns, nb, k, ts),
        out_shape=(
            jax.ShapeDtypeStruct(blk, F32),
            jax.ShapeDtypeStruct((nb, ts), F32),
            jax.ShapeDtypeStruct((k // 2, 2 * k), F32),
        ),
        in_specs=[smem, smem, smem, pl.BlockSpec(memory_space=pl.ANY), vmem],
        out_specs=(vmem, vmem, vmem),
        scratch_shapes=[
            pltpu.VMEM((n, ns * ts, ts), BF),
            pltpu.VMEM((n,) + blk, BF),
            pltpu.VMEM((n, nb, ts), F32),
            pltpu.VMEM((n, nb, ts), F32),
            pltpu.VMEM((n, nb, ts), F32),
            pltpu.VMEM(blk, F32),
            pltpu.VMEM((2, no, nc) + blk, BF),
            pltpu.VMEM((no, nc) + blk, BF),
            pltpu.VMEM((no, nc) + blk, BF),
            pltpu.VMEM((no, nc) + blk, BF),
            pltpu.VMEM((no,) + blk, BF),
            pltpu.VMEM((no,) + blk, BF),
            pltpu.VMEM((nb * k, ts), F32),
            pltpu.VMEM((ni, k // 2, 2 * k), F32),
            pltpu.VMEM((no, k // 2, 2 * k), F32),
            dma((no,)),
            dma((no,)), dma((no,)),
            dma((no, nc)), dma((no, nc)),
            dma((no, nc)), dma((no, nc)),
            dma((n,)), dma((n,)),
            dma((n,)), dma((n,)),
            dma((no,)), dma((no,)),
            dma((no, nc)), dma((no, nc)),
            dma((no,)), dma((no,)),
            dma((ni,)), dma((ni,)),
            dma((no,)), dma((no,)),
        ],
        compiler_params=pltpu.CompilerParams(
            collective_id=0, has_side_effects=True, vmem_limit_bytes=60 * 2**20),
        name="exchange",
    )(tile_row, tile_col, counts, tiles.reshape(n, ns * ts, ts), vt)
    basis = pl.pallas_call(
        functools.partial(orthonormalize, k),
        out_shape=jax.ShapeDtypeStruct((nb * ts, k), F32),
        in_specs=[vmem, vmem],
        out_specs=vmem,
        name="orthonormalize",
    )(gram, img)
    return (basis, deg.reshape(nb * ts))


def solution(mesh):
    placed = (
        P(("outer", "inner"), None, None),
        P(("outer", "inner")),
        P(("outer", "inner")),
        P(("outer", "inner")),
        P(("outer", "inner"), None),
    )
    return jax.shard_map(
        shards,
        mesh=mesh,
        in_specs=placed,
        out_specs=(P(("outer", "inner"), None), P(("outer", "inner"))),
        check_vma=False,
    )
```

```python
import functools

import jax
import jax.numpy as jnp
from jax import lax
from jax.experimental import pallas as pl
from jax.experimental.pallas import tpu as pltpu
from jax.sharding import PartitionSpec as P

MESH = pl.DeviceIdType.MESH
BF = jnp.bfloat16
F32 = jnp.float32
NT = (((1,), (1,)), ((), ()))
HI = lax.Precision.HIGHEST


def exchange(
    no, ni, ns, nb, k, ts,
    row_ref, col_ref, cnt_ref, tiles_hbm, v_ref,
    img_ref, deg_ref, gram_ref,
    tiles, vall, csum, crecv, invall, own, mout, rcore, asum, rplane, bsum, rz, fwd, ginner, gz,
    tile_sem, vz_s, vz_r, vp_s, vp_r, vc_s, vc_r, cs_s, cs_r, iv_s, iv_r,
    rc_s, rc_r, rp_s, rp_r, rz_s, rz_r, g1_s, g1_r, g2_s, g2_r,
):
    nc = ni // 2
    n = no * ni
    z = lax.axis_index("outer")
    i = lax.axis_index("inner")
    me = z * ni + i
    chip = i // 2
    core = i % 2
    sib = chip * 2 + (1 - core)

    def zof(d):
        return lax.rem(z + d, no)

    def cof(d):
        return lax.rem(chip + d, nc)

    def iof(d):
        return lax.rem(i + d, ni)

    def hof(d):
        return lax.rem(me + d, n)

    def loop(lo, hi, body):
        def step(j, carry):
            body(j)
            return carry
        lax.fori_loop(lo, hi, step, 0)

    def remote(src, dst, ssem, rsem, zz, ii):
        return pltpu.make_async_remote_copy(
            src_ref=src, dst_ref=dst, send_sem=ssem, recv_sem=rsem,
            device_id=(zz, ii), device_id_type=MESH)

    def tile_copy(q):
        part = pl.ds(q * ni, ni)
        return pltpu.make_async_copy(tiles_hbm.at[part], tiles.at[part], tile_sem.at[q])

    for q in range(no):
        tile_copy(q).start()

    barrier = pltpu.get_barrier_semaphore()

    def greet(d):
        h = hof(d)
        pl.semaphore_signal(barrier, inc=1, device_id=(h // ni, h % ni), device_id_type=MESH)
    loop(1, n, greet)
    pl.semaphore_wait(barrier, n - 1)

    def vz(d):
        return remote(vall.at[me], vall.at[me], vz_s.at[d], vz_r.at[z], zof(d), i)

    def vz_in(d):
        zz = zof(d)
        return remote(vall.at[me], vall.at[zz * ni + i], vz_s.at[d], vz_r.at[zz], zz, i)

    def vp(zd, d):
        zz = zof(zd)
        slot = vall.at[zz * ni + i]
        return remote(slot, slot, vp_s.at[zd, d], vp_r.at[zz, chip], z, cof(d) * 2 + core)

    def vp_in(zd, d):
        zz, cc = zof(zd), cof(d)
        slot = vall.at[zz * ni + cc * 2 + core]
        return remote(slot, slot, vp_s.at[zd, d], vp_r.at[zz, cc], z, cc * 2 + core)

    def vc(zd, d):
        zz, cc = zof(zd), cof(d)
        slot = vall.at[zz * ni + cc * 2 + core]
        return remote(slot, slot, vc_s.at[zd, d], vc_r.at[zz, cc], z, sib)

    def vc_in(zd, d):
        zz, cc = zof(zd), cof(d)
        slot = vall.at[zz * ni + cc * 2 + (1 - core)]
        return remote(slot, slot, vc_s.at[zd, d], vc_r.at[zz, cc], z, sib)

    for b in range(nb):
        vall[me, b] = v_ref[:, b * ts:(b + 1) * ts]

    iota8 = lax.broadcasted_iota(jnp.int32, (8, ts), 0)

    def live_index(ref, h, s):
        return jnp.where(s < cnt_ref[h], ref[h * ns + s], -1)

    def sums(h, racc):
        t = tiles[h]
        wc = jnp.concatenate(
            [jnp.where(iota8 == live_index(col_ref, h, s), 1.0, 0.0).astype(BF) for s in range(ns)], axis=1)
        csum[h] = jnp.dot(wc, t, preferred_element_type=F32)[:nb]
        for s in range(ns):
            wr = jnp.where(iota8 == live_index(row_ref, h, s), 1.0, 0.0).astype(BF)
            racc = racc + lax.dot_general(wr, t[s * ts:(s + 1) * ts], NT, preferred_element_type=F32)
        return racc

    racc = jnp.zeros((8, ts), F32)
    for q in range(no):
        tile_copy(q).wait()
        racc = lax.fori_loop(q * ni, (q + 1) * ni, sums, racc)

    def cs(d):
        h = hof(d)
        return remote(csum.at[h], crecv.at[me], cs_s.at[d], cs_r.at[me], h // ni, h % ni)

    def cs_in(d):
        h = hof(d)
        return remote(csum.at[h], crecv.at[h], cs_s.at[d], cs_r.at[h], h // ni, h % ni)

    loop(1, n, lambda d: cs(d).start())

    loop(1, no, lambda d: vz(d).start())
    loop(1, nc, lambda d: vp(0, d).start())
    vc(0, 0).start()

    def add_sums(d, acc):
        cs_in(d).wait_recv()
        return acc + crecv[hof(d)]
    degree = lax.fori_loop(1, n, add_sums, 1.0 + racc[:nb] + csum[me])
    deg_ref[...] = degree
    invall[me] = lax.rsqrt(degree)

    def iv(d):
        h = hof(d)
        return remote(invall.at[me], invall.at[me], iv_s.at[d], iv_r.at[me], h // ni, h % ni)

    def iv_in(d):
        h = hof(d)
        return remote(invall.at[h], invall.at[h], iv_s.at[d], iv_r.at[h], h // ni, h % ni)

    loop(1, n, lambda d: iv(d).start())

    inv = invall[me]
    for b in range(nb):
        own[b] = (inv[b:b + 1] * vall[me, b].astype(F32)).astype(BF).astype(F32)

    def mirror(zz, cc, half):
        h = zz * ni + cc * 2 + half
        parts = [[] for _ in range(nb)]
        for s in range(ns):
            c = live_index(col_ref, h, s)
            rows = own[row_ref[h * ns + s]]
            for b in range(nb):
                parts[b].append((rows * jnp.where(c == b, 1.0, 0.0)).astype(BF))
        left = jnp.concatenate([jnp.concatenate(p, axis=1) for p in parts], axis=0)
        m = jnp.dot(left, tiles[h], preferred_element_type=F32)
        mout[half, zz, cc] = m.astype(BF).reshape(nb, k, ts)

    def rc(zd):
        zz = zof(zd)
        return remote(mout.at[1 - core, zz], rcore.at[zz], rc_s.at[zz], rc_r.at[zz], z, sib)

    def rp(zd, d):
        zz, cc = zof(zd), cof(d)
        return remote(asum.at[zz, cc], rplane.at[zz, chip], rp_s.at[zd, d], rp_r.at[zz, chip], z, cc * 2 + core)

    def rp_in(zd, d):
        zz, cc = zof(zd), cof(d)
        return remote(asum.at[zz, cc], rplane.at[zz, cc], rp_s.at[zd, d], rp_r.at[zz, cc], z, cc * 2 + core)

    def rzc(zd):
        return remote(bsum.at[zof(zd)], rz.at[z], rz_s.at[zd], rz_r.at[z], zof(zd), i)

    def rz_in(zd):
        zz = zof(zd)
        return remote(bsum.at[zz], rz.at[zz], rz_s.at[zd], rz_r.at[zz], zz, i)

    def make_chunk(zo):
        zd = lax.rem(zo + 1, no)
        zz = zof(zd)
        loop(0, nc, lambda cc: mirror(zz, cc, 1 - core))
        rc(zd).start()
        loop(0, nc, lambda cc: mirror(zz, cc, core))
    loop(0, no, make_chunk)

    def relay_z(zd):
        vz_in(zd).wait_recv()
        loop(1, nc, lambda d: vp(zd, d).start())
        vc(zd, 0).start()
    loop(1, no, relay_z)

    def send_chunk(zo):
        zd = lax.rem(zo + 1, no)
        zz = zof(zd)
        rc(zd).wait_recv()

        def add_one(d):
            cc = cof(d)
            asum[zz, cc] = (mout[core, zz, cc].astype(F32) + rcore[zz, cc].astype(F32)).astype(BF)

        def add_send(d):
            add_one(d)
            rp(zd, d).start()
        loop(1, nc, add_send)
        add_one(0)
    loop(0, no, send_chunk)

    def relay_p(zd):
        def one(d):
            vp_in(zd, d).wait_recv()
            vc(zd, d).start()
        loop(1, nc, one)
    loop(0, no, relay_p)
    loop(1, n, lambda d: iv_in(d).wait_recv())
    loop(0, no, lambda zd: loop(0, nc, lambda d: vc_in(zd, d).wait_recv()))

    fwd[...] = jnp.zeros_like(fwd)

    def forward(h):
        acc = fwd[...]
        for s in range(ns):
            c = col_ref[h * ns + s]
            r = live_index(row_ref, h, s)
            blk = (inv_row(h, c) * vall[h, c].astype(F32)).astype(BF).astype(F32)
            left = jnp.concatenate([(blk * jnp.where(r == b, 1.0, 0.0)).astype(BF) for b in range(nb)], axis=0)
            acc = acc + lax.dot_general(left, tiles[h, s * ts:(s + 1) * ts], NT, preferred_element_type=F32)
        fwd[...] = acc

    def inv_row(h, c):
        rows = invall[h]
        out = rows[0:1]
        for b in range(1, nb):
            out = jnp.where(jnp.broadcast_to(c, out.shape) == b, rows[b:b + 1], out)
        return out

    def work(zo):
        zd = lax.rem(zo + 1, no)
        zz = zof(zd)
        loop(zz * ni, (zz + 1) * ni, forward)
        total = asum[zz, chip].astype(F32)

        def add_p(d, acc):
            rp_in(zd, d).wait_recv()
            return acc + rplane[zz, cof(d)].astype(F32)
        total = lax.fori_loop(1, nc, add_p, total)
        bsum[zz] = total.astype(BF)

    def work_send(zo):
        work(zo)
        rzc(lax.rem(zo + 1, no)).start()
    loop(0, no - 1, work_send)
    work(no - 1)

    def add_z(d, acc):
        rz_in(d).wait_recv()
        return acc + rz[zof(d)].astype(F32)
    total = lax.fori_loop(1, no, add_z, bsum[z].astype(F32))
    gram = jnp.zeros((k, k), F32)
    for b in range(nb):
        x = inv[b:b + 1] * (total[b] + fwd[b * k:(b + 1) * k] + own[b])
        img_ref[b] = x
        gram = gram + lax.dot_general(x, x, NT, preferred_element_type=F32, precision=HI)
    half = k // 2
    ginner[i] = jnp.concatenate([gram[:half], gram[half:]], axis=1)

    def g1(d):
        return remote(ginner.at[i], ginner.at[i], g1_s.at[d], g1_r.at[i], z, iof(d))

    def g1_in(d):
        ii = iof(d)
        return remote(ginner.at[ii], ginner.at[ii], g1_s.at[d], g1_r.at[ii], z, ii)

    def g2(d):
        return remote(gz.at[z], gz.at[z], g2_s.at[d], g2_r.at[z], zof(d), i)

    def g2_in(d):
        zz = zof(d)
        return remote(gz.at[zz], gz.at[zz], g2_s.at[d], g2_r.at[zz], zz, i)

    loop(1, ni, lambda d: g1(d).start())
    loop(1, ni, lambda d: g1_in(d).wait_recv())
    gz[z] = lax.fori_loop(1, ni, lambda j, a: a + ginner[j], ginner[0])
    loop(1, no, lambda d: g2(d).start())
    loop(1, no, lambda d: g2_in(d).wait_recv())
    g = lax.fori_loop(1, no, lambda j, a: a + gz[j], gz[0])
    gram_ref[...] = g * (1.0 / (n * nb * ts))

    loop(1, no, lambda d: vz(d).wait_send())
    loop(0, no, lambda zd: loop(1, nc, lambda d: vp(zd, d).wait_send()))
    loop(0, no, lambda zd: loop(0, nc, lambda d: vc(zd, d).wait_send()))
    loop(1, n, lambda d: cs(d).wait_send())
    loop(1, n, lambda d: iv(d).wait_send())
    loop(0, no, lambda zd: rc(zd).wait_send())
    loop(0, no, lambda zd: loop(1, nc, lambda d: rp(zd, d).wait_send()))
    loop(1, no, lambda zd: rzc(zd).wait_send())
    loop(1, ni, lambda d: g1(d).wait_send())
    loop(1, no, lambda d: g2(d).wait_send())


def orthonormalize(k, gram_ref, img_ref, deg_ref, out_ref, deg_out):
    deg_out[...] = deg_ref[...]
    g = gram_ref[...]
    a = jnp.concatenate([g[:, :k], g[:, k:]], axis=0)
    row = lax.broadcasted_iota(jnp.int32, (k, k), 0)
    col = lax.broadcasted_iota(jnp.int32, (k, k), 1)
    a = jnp.concatenate([a, jnp.where(row == col, 1.0, 0.0)], axis=1)
    rows = lax.broadcasted_iota(jnp.int32, (k, 2 * k), 0)
    scale = jnp.zeros((k, 2 * k), F32)
    for j in range(k):
        c = jnp.broadcast_to(a[:, j:j + 1], (k, 2 * k))
        piv = c[j:j + 1]
        scale = jnp.where(rows == j, c, scale)
        a = a - jnp.where(rows > j, c, 0.0) * (a[j:j + 1] / piv)
    inv_low = (a * lax.rsqrt(scale))[:, k:]
    for b in range(img_ref.shape[0]):
        ts = img_ref.shape[2]
        out_ref[:, b * ts:(b + 1) * ts] = jnp.dot(
            inv_low, img_ref[b], preferred_element_type=F32, precision=HI)


def shards(tiles, tile_row, tile_col, counts, vectors):
    no, ni = lax.axis_size("outer"), lax.axis_size("inner")
    n = no * ni
    nc = ni // 2
    ns = tiles.shape[0] // n
    ts = tiles.shape[1]
    k = vectors.shape[1]
    nb = vectors.shape[0] // ts
    dma = pltpu.SemaphoreType.DMA
    blk = (nb, k, ts)
    vmem = pl.BlockSpec(memory_space=pltpu.VMEM)
    smem = pl.BlockSpec(memory_space=pltpu.SMEM)
    img, deg, gram = pl.pallas_call(
        functools.partial(exchange, no, ni, ns, nb, k, ts),
        out_shape=(
            jax.ShapeDtypeStruct(blk, F32),
            jax.ShapeDtypeStruct((nb, ts), F32),
            jax.ShapeDtypeStruct((k // 2, 2 * k), F32),
        ),
        in_specs=[smem, smem, smem, pl.BlockSpec(memory_space=pl.ANY), vmem],
        out_specs=(vmem, vmem, vmem),
        scratch_shapes=[
            pltpu.VMEM((n, ns * ts, ts), BF),
            pltpu.VMEM((n,) + blk, BF),
            pltpu.VMEM((n, nb, ts), F32),
            pltpu.VMEM((n, nb, ts), F32),
            pltpu.VMEM((n, nb, ts), F32),
            pltpu.VMEM(blk, F32),
            pltpu.VMEM((2, no, nc) + blk, BF),
            pltpu.VMEM((no, nc) + blk, BF),
            pltpu.VMEM((no, nc) + blk, BF),
            pltpu.VMEM((no, nc) + blk, BF),
            pltpu.VMEM((no,) + blk, BF),
            pltpu.VMEM((no,) + blk, BF),
            pltpu.VMEM((nb * k, ts), F32),
            pltpu.VMEM((ni, k // 2, 2 * k), F32),
            pltpu.VMEM((no, k // 2, 2 * k), F32),
            dma((no,)),
            dma((no,)), dma((no,)),
            dma((no, nc)), dma((no, nc)),
            dma((no, nc)), dma((no, nc)),
            dma((n,)), dma((n,)),
            dma((n,)), dma((n,)),
            dma((no,)), dma((no,)),
            dma((no, nc)), dma((no, nc)),
            dma((no,)), dma((no,)),
            dma((ni,)), dma((ni,)),
            dma((no,)), dma((no,)),
        ],
        compiler_params=pltpu.CompilerParams(
            collective_id=0, has_side_effects=True, vmem_limit_bytes=60 * 2**20),
        name="exchange",
    )(tile_row, tile_col, counts, tiles.reshape(n, ns * ts, ts), vectors.T)
    basis, deg = pl.pallas_call(
        functools.partial(orthonormalize, k),
        out_shape=(
            jax.ShapeDtypeStruct((k, nb * ts), F32),
            jax.ShapeDtypeStruct((nb, ts), F32),
        ),
        in_specs=[vmem, vmem, vmem],
        out_specs=(vmem, vmem),
        name="orthonormalize",
    )(gram, img, deg)
    return (basis.T, deg.reshape(nb * ts))


def solution(mesh):
    placed = (
        P(("outer", "inner"), None, None),
        P(("outer", "inner")),
        P(("outer", "inner")),
        P(("outer", "inner")),
        P(("outer", "inner"), None),
    )
    return jax.shard_map(
        shards,
        mesh=mesh,
        in_specs=placed,
        out_specs=(P(("outer", "inner"), None), P(("outer", "inner"))),
        check_vma=False,
    )
```

```python
import functools

import jax
import jax.numpy as jnp
from jax import lax
from jax.experimental import pallas as pl
from jax.experimental.pallas import tpu as pltpu
from jax.sharding import PartitionSpec as P

MESH = pl.DeviceIdType.MESH
BF = jnp.bfloat16
F32 = jnp.float32
NT = (((1,), (1,)), ((), ()))
HI = lax.Precision.HIGHEST


def exchange(
    no, ni, ns, nb, k, ts,
    row_ref, col_ref, cnt_ref, tiles_hbm, v_ref,
    img_ref, deg_ref, gram_ref,
    tiles, vall, csum, crecv, invall, own, mout, rcore, asum, rplane, bsum, rz, fwd, ginner, gz,
    tile_sem, vz_s, vz_r, vp_s, vp_r, vc_s, vc_r, cs_s, cs_r, iv_s, iv_r,
    rc_s, rc_r, rp_s, rp_r, rz_s, rz_r, g1_s, g1_r, g2_s, g2_r,
):
    nc = ni // 2
    n = no * ni
    z = lax.axis_index("outer")
    i = lax.axis_index("inner")
    me = z * ni + i
    chip = i // 2
    core = i % 2
    sib = chip * 2 + (1 - core)

    def zof(d):
        return lax.rem(z + d, no)

    def cof(d):
        return lax.rem(chip + d, nc)

    def iof(d):
        return lax.rem(i + d, ni)

    def hof(d):
        return lax.rem(me + d, n)

    def loop(lo, hi, body):
        def step(j, carry):
            body(j)
            return carry
        lax.fori_loop(lo, hi, step, 0)

    def remote(src, dst, ssem, rsem, zz, ii):
        return pltpu.make_async_remote_copy(
            src_ref=src, dst_ref=dst, send_sem=ssem, recv_sem=rsem,
            device_id=(zz, ii), device_id_type=MESH)

    def tile_copy(q):
        part = pl.ds(q * ni, ni)
        return pltpu.make_async_copy(tiles_hbm.at[part], tiles.at[part], tile_sem.at[q])

    for q in range(no):
        tile_copy(q).start()

    barrier = pltpu.get_barrier_semaphore()

    def greet(d):
        h = hof(d)
        pl.semaphore_signal(barrier, inc=1, device_id=(h // ni, h % ni), device_id_type=MESH)
    loop(1, n, greet)
    pl.semaphore_wait(barrier, n - 1)

    def vz(d):
        return remote(vall.at[me], vall.at[me], vz_s.at[d], vz_r.at[z], zof(d), i)

    def vz_in(d):
        zz = zof(d)
        return remote(vall.at[me], vall.at[zz * ni + i], vz_s.at[d], vz_r.at[zz], zz, i)

    def vp(zd, d):
        zz = zof(zd)
        slot = vall.at[zz * ni + i]
        return remote(slot, slot, vp_s.at[zd, d], vp_r.at[zz, chip], z, cof(d) * 2 + core)

    def vp_in(zd, d):
        zz, cc = zof(zd), cof(d)
        slot = vall.at[zz * ni + cc * 2 + core]
        return remote(slot, slot, vp_s.at[zd, d], vp_r.at[zz, cc], z, cc * 2 + core)

    def vc(zd, d):
        zz, cc = zof(zd), cof(d)
        slot = vall.at[zz * ni + cc * 2 + core]
        return remote(slot, slot, vc_s.at[zd, d], vc_r.at[zz, cc], z, sib)

    def vc_in(zd, d):
        zz, cc = zof(zd), cof(d)
        slot = vall.at[zz * ni + cc * 2 + (1 - core)]
        return remote(slot, slot, vc_s.at[zd, d], vc_r.at[zz, cc], z, sib)

    for b in range(nb):
        vall[me, b] = v_ref[:, b * ts:(b + 1) * ts]
    loop(1, no, lambda d: vz(d).start())
    loop(1, nc, lambda d: vp(0, d).start())
    vc(0, 0).start()

    iota8 = lax.broadcasted_iota(jnp.int32, (8, ts), 0)

    def live_index(ref, h, s):
        return jnp.where(s < cnt_ref[h], ref[h * ns + s], -1)

    def sums(h, racc):
        t = tiles[h]
        wc = jnp.concatenate(
            [jnp.where(iota8 == live_index(col_ref, h, s), 1.0, 0.0).astype(BF) for s in range(ns)], axis=1)
        csum[h] = jnp.dot(wc, t, preferred_element_type=F32)[:nb]
        for s in range(ns):
            wr = jnp.where(iota8 == live_index(row_ref, h, s), 1.0, 0.0).astype(BF)
            racc = racc + lax.dot_general(wr, t[s * ts:(s + 1) * ts], NT, preferred_element_type=F32)
        return racc

    racc = jnp.zeros((8, ts), F32)
    for q in range(no):
        tile_copy(q).wait()
        racc = lax.fori_loop(q * ni, (q + 1) * ni, sums, racc)

    def cs(d):
        h = hof(d)
        return remote(csum.at[h], crecv.at[me], cs_s.at[d], cs_r.at[me], h // ni, h % ni)

    def cs_in(d):
        h = hof(d)
        return remote(csum.at[h], crecv.at[h], cs_s.at[d], cs_r.at[h], h // ni, h % ni)

    loop(1, n, lambda d: cs(d).start())

    def relay_z(zd):
        vz_in(zd).wait_recv()
        loop(1, nc, lambda d: vp(zd, d).start())
        vc(zd, 0).start()
    loop(1, no, relay_z)

    def add_sums(d, acc):
        cs_in(d).wait_recv()
        return acc + crecv[hof(d)]
    degree = lax.fori_loop(1, n, add_sums, 1.0 + racc[:nb] + csum[me])
    deg_ref[...] = degree
    invall[me] = lax.rsqrt(degree)

    def iv(d):
        h = hof(d)
        return remote(invall.at[me], invall.at[me], iv_s.at[d], iv_r.at[me], h // ni, h % ni)

    def iv_in(d):
        h = hof(d)
        return remote(invall.at[h], invall.at[h], iv_s.at[d], iv_r.at[h], h // ni, h % ni)

    loop(1, n, lambda d: iv(d).start())

    inv = invall[me]
    for b in range(nb):
        own[b] = (inv[b:b + 1] * vall[me, b].astype(F32)).astype(BF).astype(F32)

    def mirror(zz, cc, half):
        h = zz * ni + cc * 2 + half
        parts = [[] for _ in range(nb)]
        for s in range(ns):
            c = live_index(col_ref, h, s)
            rows = own[row_ref[h * ns + s]]
            for b in range(nb):
                parts[b].append((rows * jnp.where(c == b, 1.0, 0.0)).astype(BF))
        left = jnp.concatenate([jnp.concatenate(p, axis=1) for p in parts], axis=0)
        m = jnp.dot(left, tiles[h], preferred_element_type=F32)
        mout[half, zz, cc] = m.astype(BF).reshape(nb, k, ts)

    def rc(zd):
        zz = zof(zd)
        return remote(mout.at[1 - core, zz], rcore.at[zz], rc_s.at[zz], rc_r.at[zz], z, sib)

    def rp(zd, d):
        zz, cc = zof(zd), cof(d)
        return remote(asum.at[zz, cc], rplane.at[zz, chip], rp_s.at[zd, d], rp_r.at[zz, chip], z, cc * 2 + core)

    def rp_in(zd, d):
        zz, cc = zof(zd), cof(d)
        return remote(asum.at[zz, cc], rplane.at[zz, cc], rp_s.at[zd, d], rp_r.at[zz, cc], z, cc * 2 + core)

    def rzc(zd):
        return remote(bsum.at[zof(zd)], rz.at[z], rz_s.at[zd], rz_r.at[z], zof(zd), i)

    def rz_in(zd):
        zz = zof(zd)
        return remote(bsum.at[zz], rz.at[zz], rz_s.at[zd], rz_r.at[zz], zz, i)

    def make_chunk(zo):
        zd = lax.rem(zo + 1, no)
        zz = zof(zd)
        loop(0, nc, lambda cc: mirror(zz, cc, 1 - core))
        rc(zd).start()
        loop(0, nc, lambda cc: mirror(zz, cc, core))
    loop(0, no, make_chunk)

    def send_chunk(zo):
        zd = lax.rem(zo + 1, no)
        zz = zof(zd)
        rc(zd).wait_recv()

        def add_one(d):
            cc = cof(d)
            asum[zz, cc] = (mout[core, zz, cc].astype(F32) + rcore[zz, cc].astype(F32)).astype(BF)

        def add_send(d):
            add_one(d)
            rp(zd, d).start()
        loop(1, nc, add_send)
        add_one(0)
    loop(0, no, send_chunk)

    def relay_p(zd):
        def one(d):
            vp_in(zd, d).wait_recv()
            vc(zd, d).start()
        loop(1, nc, one)
    loop(0, no, relay_p)
    loop(1, n, lambda d: iv_in(d).wait_recv())
    loop(0, no, lambda zd: loop(0, nc, lambda d: vc_in(zd, d).wait_recv()))

    fwd[...] = jnp.zeros_like(fwd)

    def forward(h):
        acc = fwd[...]
        for s in range(ns):
            c = col_ref[h * ns + s]
            r = live_index(row_ref, h, s)
            blk = (inv_row(h, c) * vall[h, c].astype(F32)).astype(BF).astype(F32)
            left = jnp.concatenate([(blk * jnp.where(r == b, 1.0, 0.0)).astype(BF) for b in range(nb)], axis=0)
            acc = acc + lax.dot_general(left, tiles[h, s * ts:(s + 1) * ts], NT, preferred_element_type=F32)
        fwd[...] = acc

    def inv_row(h, c):
        rows = invall[h]
        out = rows[0:1]
        for b in range(1, nb):
            out = jnp.where(jnp.broadcast_to(c, out.shape) == b, rows[b:b + 1], out)
        return out

    def work(zo):
        zd = lax.rem(zo + 1, no)
        zz = zof(zd)
        loop(zz * ni, (zz + 1) * ni, forward)
        total = asum[zz, chip].astype(F32)

        def add_p(d, acc):
            rp_in(zd, d).wait_recv()
            return acc + rplane[zz, cof(d)].astype(F32)
        total = lax.fori_loop(1, nc, add_p, total)
        bsum[zz] = total.astype(BF)

    def work_send(zo):
        work(zo)
        rzc(lax.rem(zo + 1, no)).start()
    loop(0, no - 1, work_send)
    work(no - 1)

    def add_z(d, acc):
        rz_in(d).wait_recv()
        return acc + rz[zof(d)].astype(F32)
    total = lax.fori_loop(1, no, add_z, bsum[z].astype(F32))
    gram = jnp.zeros((k, k), F32)
    for b in range(nb):
        x = inv[b:b + 1] * (total[b] + fwd[b * k:(b + 1) * k] + own[b])
        img_ref[b] = x
        gram = gram + lax.dot_general(x, x, NT, preferred_element_type=F32, precision=HI)
    half = k // 2
    ginner[i] = jnp.concatenate([gram[:half], gram[half:]], axis=1)

    def g1(d):
        return remote(ginner.at[i], ginner.at[i], g1_s.at[d], g1_r.at[i], z, iof(d))

    def g1_in(d):
        ii = iof(d)
        return remote(ginner.at[ii], ginner.at[ii], g1_s.at[d], g1_r.at[ii], z, ii)

    def g2(d):
        return remote(gz.at[z], gz.at[z], g2_s.at[d], g2_r.at[z], zof(d), i)

    def g2_in(d):
        zz = zof(d)
        return remote(gz.at[zz], gz.at[zz], g2_s.at[d], g2_r.at[zz], zz, i)

    loop(1, ni, lambda d: g1(d).start())
    loop(1, ni, lambda d: g1_in(d).wait_recv())
    gz[z] = lax.fori_loop(1, ni, lambda j, a: a + ginner[j], ginner[0])
    loop(1, no, lambda d: g2(d).start())
    loop(1, no, lambda d: g2_in(d).wait_recv())
    g = lax.fori_loop(1, no, lambda j, a: a + gz[j], gz[0])
    gram_ref[...] = g * (1.0 / (n * nb * ts))

    loop(1, no, lambda d: vz(d).wait_send())
    loop(0, no, lambda zd: loop(1, nc, lambda d: vp(zd, d).wait_send()))
    loop(0, no, lambda zd: loop(0, nc, lambda d: vc(zd, d).wait_send()))
    loop(1, n, lambda d: cs(d).wait_send())
    loop(1, n, lambda d: iv(d).wait_send())
    loop(0, no, lambda zd: rc(zd).wait_send())
    loop(0, no, lambda zd: loop(1, nc, lambda d: rp(zd, d).wait_send()))
    loop(1, no, lambda zd: rzc(zd).wait_send())
    loop(1, ni, lambda d: g1(d).wait_send())
    loop(1, no, lambda d: g2(d).wait_send())


def orthonormalize(k, gram_ref, img_ref, deg_ref, out_ref, deg_out):
    deg_out[...] = deg_ref[...]
    g = gram_ref[...]
    a = jnp.concatenate([g[:, :k], g[:, k:]], axis=0)
    row = lax.broadcasted_iota(jnp.int32, (k, k), 0)
    col = lax.broadcasted_iota(jnp.int32, (k, k), 1)
    a = jnp.concatenate([a, jnp.where(row == col, 1.0, 0.0)], axis=1)
    rows = lax.broadcasted_iota(jnp.int32, (k, 2 * k), 0)
    scale = jnp.zeros((k, 2 * k), F32)
    for j in range(k):
        c = jnp.broadcast_to(a[:, j:j + 1], (k, 2 * k))
        piv = c[j:j + 1]
        scale = jnp.where(rows == j, c, scale)
        a = a - jnp.where(rows > j, c, 0.0) * (a[j:j + 1] / piv)
    inv_low = (a * lax.rsqrt(scale))[:, k:]
    for b in range(img_ref.shape[0]):
        ts = img_ref.shape[2]
        out_ref[:, b * ts:(b + 1) * ts] = jnp.dot(
            inv_low, img_ref[b], preferred_element_type=F32, precision=HI)


def shards(tiles, tile_row, tile_col, counts, vectors):
    no, ni = lax.axis_size("outer"), lax.axis_size("inner")
    n = no * ni
    nc = ni // 2
    ns = tiles.shape[0] // n
    ts = tiles.shape[1]
    k = vectors.shape[1]
    nb = vectors.shape[0] // ts
    dma = pltpu.SemaphoreType.DMA
    blk = (nb, k, ts)
    vmem = pl.BlockSpec(memory_space=pltpu.VMEM)
    smem = pl.BlockSpec(memory_space=pltpu.SMEM)
    img, deg, gram = pl.pallas_call(
        functools.partial(exchange, no, ni, ns, nb, k, ts),
        out_shape=(
            jax.ShapeDtypeStruct(blk, F32),
            jax.ShapeDtypeStruct((nb, ts), F32),
            jax.ShapeDtypeStruct((k // 2, 2 * k), F32),
        ),
        in_specs=[smem, smem, smem, pl.BlockSpec(memory_space=pl.ANY), vmem],
        out_specs=(vmem, vmem, vmem),
        scratch_shapes=[
            pltpu.VMEM((n, ns * ts, ts), BF),
            pltpu.VMEM((n,) + blk, BF),
            pltpu.VMEM((n, nb, ts), F32),
            pltpu.VMEM((n, nb, ts), F32),
            pltpu.VMEM((n, nb, ts), F32),
            pltpu.VMEM(blk, F32),
            pltpu.VMEM((2, no, nc) + blk, BF),
            pltpu.VMEM((no, nc) + blk, BF),
            pltpu.VMEM((no, nc) + blk, BF),
            pltpu.VMEM((no, nc) + blk, BF),
            pltpu.VMEM((no,) + blk, BF),
            pltpu.VMEM((no,) + blk, BF),
            pltpu.VMEM((nb * k, ts), F32),
            pltpu.VMEM((ni, k // 2, 2 * k), F32),
            pltpu.VMEM((no, k // 2, 2 * k), F32),
            dma((no,)),
            dma((no,)), dma((no,)),
            dma((no, nc)), dma((no, nc)),
            dma((no, nc)), dma((no, nc)),
            dma((n,)), dma((n,)),
            dma((n,)), dma((n,)),
            dma((no,)), dma((no,)),
            dma((no, nc)), dma((no, nc)),
            dma((no,)), dma((no,)),
            dma((ni,)), dma((ni,)),
            dma((no,)), dma((no,)),
        ],
        compiler_params=pltpu.CompilerParams(
            collective_id=0, has_side_effects=True, vmem_limit_bytes=60 * 2**20),
        name="exchange",
    )(tile_row, tile_col, counts, tiles.reshape(n, ns * ts, ts), vectors.T)
    basis, deg = pl.pallas_call(
        functools.partial(orthonormalize, k),
        out_shape=(
            jax.ShapeDtypeStruct((k, nb * ts), F32),
            jax.ShapeDtypeStruct((nb, ts), F32),
        ),
        in_specs=[vmem, vmem, vmem],
        out_specs=(vmem, vmem),
        name="orthonormalize",
    )(gram, img, deg)
    return (basis.T, deg.reshape(nb * ts))


def solution(mesh):
    placed = (
        P(("outer", "inner"), None, None),
        P(("outer", "inner")),
        P(("outer", "inner")),
        P(("outer", "inner")),
        P(("outer", "inner"), None),
    )
    return jax.shard_map(
        shards,
        mesh=mesh,
        in_specs=placed,
        out_specs=(P(("outer", "inner"), None), P(("outer", "inner"))),
        check_vma=False,
    )
```

```python
import functools

import jax
import jax.numpy as jnp
from jax import lax
from jax.experimental import pallas as pl
from jax.experimental.pallas import tpu as pltpu
from jax.sharding import PartitionSpec as P

MESH = pl.DeviceIdType.MESH
BF = jnp.bfloat16
F32 = jnp.float32
NT = (((1,), (1,)), ((), ()))
HI = lax.Precision.HIGHEST


def exchange(
    no, ni, ns, nb, k, ts,
    row_ref, col_ref, cnt_ref, tiles_hbm, v_ref,
    img_ref, deg_ref, gram_ref,
    tiles, vall, csum, crecv, invall, own, mout, rcore, asum, rplane, bsum, rz, fwd, ginner, gz,
    tile_sem, vz_s, vz_r, vp_s, vp_r, vc_s, vc_r, cs_s, cs_r, iv_s, iv_r,
    rc_s, rc_r, rp_s, rp_r, rz_s, rz_r, g1_s, g1_r, g2_s, g2_r,
):
    nc = ni // 2
    n = no * ni
    z = lax.axis_index("outer")
    i = lax.axis_index("inner")
    me = z * ni + i
    chip = i // 2
    core = i % 2
    sib = chip * 2 + (1 - core)

    def zof(d):
        return lax.rem(z + d, no)

    def cof(d):
        return lax.rem(chip + d, nc)

    def iof(d):
        return lax.rem(i + d, ni)

    def hof(d):
        return lax.rem(me + d, n)

    def loop(lo, hi, body):
        def step(j, carry):
            body(j)
            return carry
        lax.fori_loop(lo, hi, step, 0)

    def remote(src, dst, ssem, rsem, zz, ii):
        return pltpu.make_async_remote_copy(
            src_ref=src, dst_ref=dst, send_sem=ssem, recv_sem=rsem,
            device_id=(zz, ii), device_id_type=MESH)

    def tile_copy(q):
        part = pl.ds(q * ni, ni)
        return pltpu.make_async_copy(tiles_hbm.at[part], tiles.at[part], tile_sem.at[q])

    for q in range(no):
        tile_copy(q).start()

    barrier = pltpu.get_barrier_semaphore()

    def greet(d):
        h = hof(d)
        pl.semaphore_signal(barrier, inc=1, device_id=(h // ni, h % ni), device_id_type=MESH)
    loop(1, n, greet)
    pl.semaphore_wait(barrier, n - 1)

    def vz(d):
        return remote(vall.at[me], vall.at[me], vz_s.at[d], vz_r.at[z], zof(d), i)

    def vz_in(d):
        zz = zof(d)
        return remote(vall.at[me], vall.at[zz * ni + i], vz_s.at[d], vz_r.at[zz], zz, i)

    def vp(zd, d):
        zz = zof(zd)
        slot = vall.at[zz * ni + i]
        return remote(slot, slot, vp_s.at[zd, d], vp_r.at[zz, chip], z, cof(d) * 2 + core)

    def vp_in(zd, d):
        zz, cc = zof(zd), cof(d)
        slot = vall.at[zz * ni + cc * 2 + core]
        return remote(slot, slot, vp_s.at[zd, d], vp_r.at[zz, cc], z, cc * 2 + core)

    def vc(zd, d):
        zz, cc = zof(zd), cof(d)
        slot = vall.at[zz * ni + cc * 2 + core]
        return remote(slot, slot, vc_s.at[zd, d], vc_r.at[zz, cc], z, sib)

    def vc_in(zd, d):
        zz, cc = zof(zd), cof(d)
        slot = vall.at[zz * ni + cc * 2 + (1 - core)]
        return remote(slot, slot, vc_s.at[zd, d], vc_r.at[zz, cc], z, sib)

    for b in range(nb):
        vall[me, b] = v_ref[:, b * ts:(b + 1) * ts]
    loop(1, no, lambda d: vz(d).start())
    loop(1, nc, lambda d: vp(0, d).start())
    vc(0, 0).start()

    iota8 = lax.broadcasted_iota(jnp.int32, (8, ts), 0)

    def live_index(ref, h, s):
        return jnp.where(s < cnt_ref[h], ref[h * ns + s], -1)

    def sums(h, racc):
        t = tiles[h]
        wc = jnp.concatenate(
            [jnp.where(iota8 == live_index(col_ref, h, s), 1.0, 0.0).astype(BF) for s in range(ns)], axis=1)
        csum[h] = jnp.dot(wc, t, preferred_element_type=F32)[:nb]
        for s in range(ns):
            wr = jnp.where(iota8 == live_index(row_ref, h, s), 1.0, 0.0).astype(BF)
            racc = racc + lax.dot_general(wr, t[s * ts:(s + 1) * ts], NT, preferred_element_type=F32)
        return racc

    racc = jnp.zeros((8, ts), F32)
    for q in range(no):
        tile_copy(q).wait()
        racc = lax.fori_loop(q * ni, (q + 1) * ni, sums, racc)

    def cs(d):
        h = hof(d)
        return remote(csum.at[h], crecv.at[me], cs_s.at[d], cs_r.at[me], h // ni, h % ni)

    def cs_in(d):
        h = hof(d)
        return remote(csum.at[h], crecv.at[h], cs_s.at[d], cs_r.at[h], h // ni, h % ni)

    loop(1, n, lambda d: cs(d).start())

    def relay_z(zd):
        vz_in(zd).wait_recv()
        loop(1, nc, lambda d: vp(zd, d).start())
        vc(zd, 0).start()
    loop(1, no, relay_z)

    def add_sums(d, acc):
        cs_in(d).wait_recv()
        return acc + crecv[hof(d)]
    degree = lax.fori_loop(1, n, add_sums, 1.0 + racc[:nb] + csum[me])
    deg_ref[...] = degree
    invall[me] = lax.rsqrt(degree)

    def iv(d):
        h = hof(d)
        return remote(invall.at[me], invall.at[me], iv_s.at[d], iv_r.at[me], h // ni, h % ni)

    def iv_in(d):
        h = hof(d)
        return remote(invall.at[h], invall.at[h], iv_s.at[d], iv_r.at[h], h // ni, h % ni)

    loop(1, n, lambda d: iv(d).start())

    inv = invall[me]
    for b in range(nb):
        own[b] = (inv[b:b + 1] * vall[me, b].astype(F32)).astype(BF).astype(F32)

    def mirror(zz, cc, half):
        h = zz * ni + cc * 2 + half
        parts = [[] for _ in range(nb)]
        for s in range(ns):
            c = live_index(col_ref, h, s)
            rows = own[row_ref[h * ns + s]]
            for b in range(nb):
                parts[b].append((rows * jnp.where(c == b, 1.0, 0.0)).astype(BF))
        left = jnp.concatenate([jnp.concatenate(p, axis=1) for p in parts], axis=0)
        m = jnp.dot(left, tiles[h], preferred_element_type=F32)
        mout[half, zz, cc] = m.astype(BF).reshape(nb, k, ts)

    def rc(zd):
        zz = zof(zd)
        return remote(mout.at[1 - core, zz], rcore.at[zz], rc_s.at[zz], rc_r.at[zz], z, sib)

    def rp(zd, d):
        zz, cc = zof(zd), cof(d)
        return remote(asum.at[zz, cc], rplane.at[zz, chip], rp_s.at[zd, d], rp_r.at[zz, chip], z, cc * 2 + core)

    def rp_in(zd, d):
        zz, cc = zof(zd), cof(d)
        return remote(asum.at[zz, cc], rplane.at[zz, cc], rp_s.at[zd, d], rp_r.at[zz, cc], z, cc * 2 + core)

    def rzc(zd):
        return remote(bsum.at[zof(zd)], rz.at[z], rz_s.at[zd], rz_r.at[z], zof(zd), i)

    def rz_in(zd):
        zz = zof(zd)
        return remote(bsum.at[zz], rz.at[zz], rz_s.at[zd], rz_r.at[zz], zz, i)

    def make_chunk(zo):
        zd = lax.rem(zo + 1, no)
        zz = zof(zd)
        loop(0, nc, lambda cc: mirror(zz, cc, 1 - core))
        rc(zd).start()
        loop(0, nc, lambda cc: mirror(zz, cc, core))
    loop(0, no, make_chunk)

    def send_chunk(zo):
        zd = lax.rem(zo + 1, no)
        zz = zof(zd)
        rc(zd).wait_recv()

        def add_one(d):
            cc = cof(d)
            asum[zz, cc] = (mout[core, zz, cc].astype(F32) + rcore[zz, cc].astype(F32)).astype(BF)

        def add_send(d):
            add_one(d)
            rp(zd, d).start()
        loop(1, nc, add_send)
        add_one(0)
    loop(0, no, send_chunk)

    def relay_p(zd):
        def one(d):
            vp_in(zd, d).wait_recv()
            vc(zd, d).start()
        loop(1, nc, one)
    loop(0, no, relay_p)
    loop(1, n, lambda d: iv_in(d).wait_recv())
    loop(0, no, lambda zd: loop(0, nc, lambda d: vc_in(zd, d).wait_recv()))

    fwd[...] = jnp.zeros_like(fwd)

    def forward(h):
        acc = fwd[...]
        for s in range(ns):
            c = col_ref[h * ns + s]
            r = live_index(row_ref, h, s)
            blk = (inv_row(h, c) * vall[h, c].astype(F32)).astype(BF).astype(F32)
            left = jnp.concatenate([(blk * jnp.where(r == b, 1.0, 0.0)).astype(BF) for b in range(nb)], axis=0)
            acc = acc + lax.dot_general(left, tiles[h, s * ts:(s + 1) * ts], NT, preferred_element_type=F32)
        fwd[...] = acc

    def inv_row(h, c):
        rows = invall[h]
        out = rows[0:1]
        for b in range(1, nb):
            out = jnp.where(jnp.broadcast_to(c, out.shape) == b, rows[b:b + 1], out)
        return out

    def work(zo):
        zd = lax.rem(zo + 1, no)
        zz = zof(zd)
        loop(zz * ni, (zz + 1) * ni, forward)
        total = asum[zz, chip].astype(F32)

        def add_p(d, acc):
            rp_in(zd, d).wait_recv()
            return acc + rplane[zz, cof(d)].astype(F32)
        total = lax.fori_loop(1, nc, add_p, total)
        bsum[zz] = total.astype(BF)

    def work_send(zo):
        work(zo)
        rzc(lax.rem(zo + 1, no)).start()
    loop(0, no - 1, work_send)
    work(no - 1)

    def add_z(d, acc):
        rz_in(d).wait_recv()
        return acc + rz[zof(d)].astype(F32)
    total = lax.fori_loop(1, no, add_z, bsum[z].astype(F32))
    gram = jnp.zeros((k, k), F32)
    for b in range(nb):
        x = inv[b:b + 1] * (total[b] + fwd[b * k:(b + 1) * k] + own[b])
        img_ref[b] = x
        gram = gram + lax.dot_general(x, x, NT, preferred_element_type=F32, precision=HI)
    half = k // 2
    ginner[i] = jnp.concatenate([gram[:half], gram[half:]], axis=1)

    def g1(d):
        return remote(ginner.at[i], ginner.at[i], g1_s.at[d], g1_r.at[i], z, iof(d))

    def g1_in(d):
        ii = iof(d)
        return remote(ginner.at[ii], ginner.at[ii], g1_s.at[d], g1_r.at[ii], z, ii)

    def g2(d):
        return remote(gz.at[z], gz.at[z], g2_s.at[d], g2_r.at[z], zof(d), i)

    def g2_in(d):
        zz = zof(d)
        return remote(gz.at[zz], gz.at[zz], g2_s.at[d], g2_r.at[zz], zz, i)

    loop(1, ni, lambda d: g1(d).start())
    loop(1, ni, lambda d: g1_in(d).wait_recv())
    gz[z] = lax.fori_loop(1, ni, lambda j, a: a + ginner[j], ginner[0])
    loop(1, no, lambda d: g2(d).start())
    loop(1, no, lambda d: g2_in(d).wait_recv())
    g = lax.fori_loop(1, no, lambda j, a: a + gz[j], gz[0])
    gram_ref[...] = g * (1.0 / (n * nb * ts))

    loop(1, no, lambda d: vz(d).wait_send())
    loop(0, no, lambda zd: loop(1, nc, lambda d: vp(zd, d).wait_send()))
    loop(0, no, lambda zd: loop(0, nc, lambda d: vc(zd, d).wait_send()))
    loop(1, n, lambda d: cs(d).wait_send())
    loop(1, n, lambda d: iv(d).wait_send())
    loop(0, no, lambda zd: rc(zd).wait_send())
    loop(0, no, lambda zd: loop(1, nc, lambda d: rp(zd, d).wait_send()))
    loop(1, no, lambda zd: rzc(zd).wait_send())
    loop(1, ni, lambda d: g1(d).wait_send())
    loop(1, no, lambda d: g2(d).wait_send())


def orthonormalize(k, gram_ref, img_ref, deg_ref, out_ref, deg_out):
    deg_out[...] = deg_ref[...]
    g = gram_ref[...]
    a = jnp.concatenate([g[:, :k], g[:, k:]], axis=0)
    row = lax.broadcasted_iota(jnp.int32, (k, k), 0)
    col = lax.broadcasted_iota(jnp.int32, (k, k), 1)
    a = jnp.concatenate([a, jnp.where(row == col, 1.0, 0.0)], axis=1)
    rows = lax.broadcasted_iota(jnp.int32, (k, 2 * k), 0)
    scale = jnp.zeros((k, 2 * k), F32)
    for j0 in range(0, k, 8):
        cols = [jnp.broadcast_to(a[:, j0 + q:j0 + q + 1], (k, 2 * k)) for q in range(8)]
        lines = [a[j0 + q:j0 + q + 1] for q in range(8)]
        for q in range(8):
            c, j = cols[q], j0 + q
            over = 1.0 / c[j:j + 1]
            line = lines[q] * over
            scale = jnp.where(rows == j, c, scale)
            for p in range(q + 1, 8):
                at = c[j0 + p:j0 + p + 1]
                lines[p] = lines[p] - at * line
                cols[p] = cols[p] - c * (at * over)
            a = a - jnp.where(rows > j, c, 0.0) * line
    inv_low = (a * lax.rsqrt(scale))[:, k:]
    for b in range(img_ref.shape[0]):
        ts = img_ref.shape[2]
        out_ref[:, b * ts:(b + 1) * ts] = jnp.dot(
            inv_low, img_ref[b], preferred_element_type=F32, precision=HI)


def shards(tiles, tile_row, tile_col, counts, vectors):
    no, ni = lax.axis_size("outer"), lax.axis_size("inner")
    n = no * ni
    nc = ni // 2
    ns = tiles.shape[0] // n
    ts = tiles.shape[1]
    k = vectors.shape[1]
    nb = vectors.shape[0] // ts
    dma = pltpu.SemaphoreType.DMA
    blk = (nb, k, ts)
    vmem = pl.BlockSpec(memory_space=pltpu.VMEM)
    smem = pl.BlockSpec(memory_space=pltpu.SMEM)
    img, deg, gram = pl.pallas_call(
        functools.partial(exchange, no, ni, ns, nb, k, ts),
        out_shape=(
            jax.ShapeDtypeStruct(blk, F32),
            jax.ShapeDtypeStruct((nb, ts), F32),
            jax.ShapeDtypeStruct((k // 2, 2 * k), F32),
        ),
        in_specs=[smem, smem, smem, pl.BlockSpec(memory_space=pl.ANY), vmem],
        out_specs=(vmem, vmem, vmem),
        scratch_shapes=[
            pltpu.VMEM((n, ns * ts, ts), BF),
            pltpu.VMEM((n,) + blk, BF),
            pltpu.VMEM((n, nb, ts), F32),
            pltpu.VMEM((n, nb, ts), F32),
            pltpu.VMEM((n, nb, ts), F32),
            pltpu.VMEM(blk, F32),
            pltpu.VMEM((2, no, nc) + blk, BF),
            pltpu.VMEM((no, nc) + blk, BF),
            pltpu.VMEM((no, nc) + blk, BF),
            pltpu.VMEM((no, nc) + blk, BF),
            pltpu.VMEM((no,) + blk, BF),
            pltpu.VMEM((no,) + blk, BF),
            pltpu.VMEM((nb * k, ts), F32),
            pltpu.VMEM((ni, k // 2, 2 * k), F32),
            pltpu.VMEM((no, k // 2, 2 * k), F32),
            dma((no,)),
            dma((no,)), dma((no,)),
            dma((no, nc)), dma((no, nc)),
            dma((no, nc)), dma((no, nc)),
            dma((n,)), dma((n,)),
            dma((n,)), dma((n,)),
            dma((no,)), dma((no,)),
            dma((no, nc)), dma((no, nc)),
            dma((no,)), dma((no,)),
            dma((ni,)), dma((ni,)),
            dma((no,)), dma((no,)),
        ],
        compiler_params=pltpu.CompilerParams(
            collective_id=0, has_side_effects=True, vmem_limit_bytes=60 * 2**20),
        name="exchange",
    )(tile_row, tile_col, counts, tiles.reshape(n, ns * ts, ts), vectors.T)
    basis, deg = pl.pallas_call(
        functools.partial(orthonormalize, k),
        out_shape=(
            jax.ShapeDtypeStruct((k, nb * ts), F32),
            jax.ShapeDtypeStruct((nb, ts), F32),
        ),
        in_specs=[vmem, vmem, vmem],
        out_specs=(vmem, vmem),
        name="orthonormalize",
    )(gram, img, deg)
    return (basis.T, deg.reshape(nb * ts))


def solution(mesh):
    placed = (
        P(("outer", "inner"), None, None),
        P(("outer", "inner")),
        P(("outer", "inner")),
        P(("outer", "inner")),
        P(("outer", "inner"), None),
    )
    return jax.shard_map(
        shards,
        mesh=mesh,
        in_specs=placed,
        out_specs=(P(("outer", "inner"), None), P(("outer", "inner"))),
        check_vma=False,
    )
```

```python
import functools

import jax
import jax.numpy as jnp
from jax import lax
from jax.experimental import pallas as pl
from jax.experimental.pallas import tpu as pltpu
from jax.sharding import PartitionSpec as P

MESH = pl.DeviceIdType.MESH
BF = jnp.bfloat16
F32 = jnp.float32
NT = (((1,), (1,)), ((), ()))
HI = lax.Precision.HIGHEST


def exchange(
    no, ni, ns, nb, k, ts,
    row_ref, col_ref, cnt_ref, tiles_hbm, v_ref,
    img_ref, deg_ref, gram_ref,
    tiles, vall, csum, crecv, invall, own, mout, rcore, asum, rplane, bsum, rz, fwd, ginner, gz,
    tile_sem, vz_s, vz_r, vp_s, vp_r, vc_s, vc_r, cs_s, cs_r, iv_s, iv_r,
    rc_s, rc_r, rp_s, rp_r, rz_s, rz_r, g1_s, g1_r, g2_s, g2_r,
):
    nc = ni // 2
    n = no * ni
    z = lax.axis_index("outer")
    i = lax.axis_index("inner")
    me = z * ni + i
    chip = i // 2
    core = i % 2
    sib = chip * 2 + (1 - core)

    def zof(d):
        return lax.rem(z + d, no)

    def cof(d):
        return lax.rem(chip + d, nc)

    def iof(d):
        return lax.rem(i + d, ni)

    def hof(d):
        return lax.rem(me + d, n)

    def loop(lo, hi, body):
        def step(j, carry):
            body(j)
            return carry
        lax.fori_loop(lo, hi, step, 0)

    def remote(src, dst, ssem, rsem, zz, ii):
        return pltpu.make_async_remote_copy(
            src_ref=src, dst_ref=dst, send_sem=ssem, recv_sem=rsem,
            device_id=(zz, ii), device_id_type=MESH)

    def tile_copy(q):
        part = pl.ds(q * ni, ni)
        return pltpu.make_async_copy(tiles_hbm.at[part], tiles.at[part], tile_sem.at[q])

    for q in range(no):
        tile_copy(q).start()

    barrier = pltpu.get_barrier_semaphore()

    def greet(d):
        h = hof(d)
        pl.semaphore_signal(barrier, inc=1, device_id=(h // ni, h % ni), device_id_type=MESH)
    loop(1, n, greet)
    pl.semaphore_wait(barrier, n - 1)

    def vz(d):
        return remote(vall.at[me], vall.at[me], vz_s.at[d], vz_r.at[z], zof(d), i)

    def vz_in(d):
        zz = zof(d)
        return remote(vall.at[me], vall.at[zz * ni + i], vz_s.at[d], vz_r.at[zz], zz, i)

    def vp(zd, d):
        zz = zof(zd)
        slot = vall.at[zz * ni + i]
        return remote(slot, slot, vp_s.at[zd, d], vp_r.at[zz, chip], z, cof(d) * 2 + core)

    def vp_in(zd, d):
        zz, cc = zof(zd), cof(d)
        slot = vall.at[zz * ni + cc * 2 + core]
        return remote(slot, slot, vp_s.at[zd, d], vp_r.at[zz, cc], z, cc * 2 + core)

    def vc(zd, d):
        zz, cc = zof(zd), cof(d)
        slot = vall.at[zz * ni + cc * 2 + core]
        return remote(slot, slot, vc_s.at[zd, d], vc_r.at[zz, cc], z, sib)

    def vc_in(zd, d):
        zz, cc = zof(zd), cof(d)
        slot = vall.at[zz * ni + cc * 2 + (1 - core)]
        return remote(slot, slot, vc_s.at[zd, d], vc_r.at[zz, cc], z, sib)

    for b in range(nb):
        vall[me, b] = v_ref[:, b * ts:(b + 1) * ts]
    loop(1, no, lambda d: vz(d).start())
    loop(1, nc, lambda d: vp(0, d).start())
    vc(0, 0).start()

    iota8 = lax.broadcasted_iota(jnp.int32, (8, ts), 0)

    def live_index(ref, h, s):
        return jnp.where(s < cnt_ref[h], ref[h * ns + s], -1)

    def sums(h, racc):
        t = tiles[h]
        wc = jnp.concatenate(
            [jnp.where(iota8 == live_index(col_ref, h, s), 1.0, 0.0).astype(BF) for s in range(ns)], axis=1)
        csum[h] = jnp.dot(wc, t, preferred_element_type=F32)[:nb]
        for s in range(ns):
            wr = jnp.where(iota8 == live_index(row_ref, h, s), 1.0, 0.0).astype(BF)
            racc = racc + lax.dot_general(wr, t[s * ts:(s + 1) * ts], NT, preferred_element_type=F32)
        return racc

    racc = jnp.zeros((8, ts), F32)
    for q in range(no):
        tile_copy(q).wait()
        racc = lax.fori_loop(q * ni, (q + 1) * ni, sums, racc)

    def cs(d):
        h = hof(d)
        return remote(csum.at[h], crecv.at[me], cs_s.at[d], cs_r.at[me], h // ni, h % ni)

    def cs_in(d):
        h = hof(d)
        return remote(csum.at[h], crecv.at[h], cs_s.at[d], cs_r.at[h], h // ni, h % ni)

    loop(1, n, lambda d: cs(d).start())

    def relay_z(zd):
        vz_in(zd).wait_recv()
        loop(1, nc, lambda d: vp(zd, d).start())
        vc(zd, 0).start()
    loop(1, no, relay_z)

    def add_sums(d, acc):
        cs_in(d).wait_recv()
        return acc + crecv[hof(d)]
    degree = lax.fori_loop(1, n, add_sums, 1.0 + racc[:nb] + csum[me])
    deg_ref[...] = degree
    invall[me] = lax.rsqrt(degree)

    def iv(d):
        h = hof(d)
        return remote(invall.at[me], invall.at[me], iv_s.at[d], iv_r.at[me], h // ni, h % ni)

    def iv_in(d):
        h = hof(d)
        return remote(invall.at[h], invall.at[h], iv_s.at[d], iv_r.at[h], h // ni, h % ni)

    loop(1, n, lambda d: iv(d).start())

    inv = invall[me]
    for b in range(nb):
        own[b] = (inv[b:b + 1] * vall[me, b].astype(F32)).astype(BF).astype(F32)

    def mirror(zz, cc, half):
        h = zz * ni + cc * 2 + half
        parts = [[] for _ in range(nb)]
        for s in range(ns):
            c = live_index(col_ref, h, s)
            rows = own[row_ref[h * ns + s]]
            for b in range(nb):
                parts[b].append((rows * jnp.where(c == b, 1.0, 0.0)).astype(BF))
        left = jnp.concatenate([jnp.concatenate(p, axis=1) for p in parts], axis=0)
        m = jnp.dot(left, tiles[h], preferred_element_type=F32)
        mout[half, zz, cc] = m.astype(BF).reshape(nb, k, ts)

    def rc(zd):
        zz = zof(zd)
        return remote(mout.at[1 - core, zz], rcore.at[zz], rc_s.at[zz], rc_r.at[zz], z, sib)

    def rp(zd, d):
        zz, cc = zof(zd), cof(d)
        return remote(asum.at[zz, cc], rplane.at[zz, chip], rp_s.at[zd, d], rp_r.at[zz, chip], z, cc * 2 + core)

    def rp_in(zd, d):
        zz, cc = zof(zd), cof(d)
        return remote(asum.at[zz, cc], rplane.at[zz, cc], rp_s.at[zd, d], rp_r.at[zz, cc], z, cc * 2 + core)

    def rzc(zd):
        return remote(bsum.at[zof(zd)], rz.at[z], rz_s.at[zd], rz_r.at[z], zof(zd), i)

    def rz_in(zd):
        zz = zof(zd)
        return remote(bsum.at[zz], rz.at[zz], rz_s.at[zd], rz_r.at[zz], zz, i)

    def make_chunk(zo):
        zd = lax.rem(zo + 1, no)
        zz = zof(zd)
        loop(0, nc, lambda cc: mirror(zz, cc, 1 - core))
        rc(zd).start()
        loop(0, nc, lambda cc: mirror(zz, cc, core))

    def send_chunk(zo):
        zd = lax.rem(zo + 1, no)
        zz = zof(zd)
        rc(zd).wait_recv()

        def add_one(d):
            cc = cof(d)
            asum[zz, cc] = (mout[core, zz, cc].astype(F32) + rcore[zz, cc].astype(F32)).astype(BF)

        def add_send(d):
            add_one(d)
            rp(zd, d).start()
        loop(1, nc, add_send)
        add_one(0)
    make_chunk(0)

    def make_send(zo):
        make_chunk(zo)
        send_chunk(zo - 1)
    loop(1, no, make_send)
    send_chunk(no - 1)

    def relay_p(zd):
        def one(d):
            vp_in(zd, d).wait_recv()
            vc(zd, d).start()
        loop(1, nc, one)
    loop(0, no, relay_p)
    loop(1, n, lambda d: iv_in(d).wait_recv())
    loop(0, no, lambda zd: loop(0, nc, lambda d: vc_in(zd, d).wait_recv()))

    fwd[...] = jnp.zeros_like(fwd)

    def forward(h):
        acc = fwd[...]
        for s in range(ns):
            c = col_ref[h * ns + s]
            r = live_index(row_ref, h, s)
            blk = (inv_row(h, c) * vall[h, c].astype(F32)).astype(BF).astype(F32)
            left = jnp.concatenate([(blk * jnp.where(r == b, 1.0, 0.0)).astype(BF) for b in range(nb)], axis=0)
            acc = acc + lax.dot_general(left, tiles[h, s * ts:(s + 1) * ts], NT, preferred_element_type=F32)
        fwd[...] = acc

    def inv_row(h, c):
        rows = invall[h]
        out = rows[0:1]
        for b in range(1, nb):
            out = jnp.where(jnp.broadcast_to(c, out.shape) == b, rows[b:b + 1], out)
        return out

    def work(zo):
        zd = lax.rem(zo + 1, no)
        zz = zof(zd)
        loop(zz * ni, (zz + 1) * ni, forward)
        total = asum[zz, chip].astype(F32)

        def add_p(d, acc):
            rp_in(zd, d).wait_recv()
            return acc + rplane[zz, cof(d)].astype(F32)
        total = lax.fori_loop(1, nc, add_p, total)
        bsum[zz] = total.astype(BF)

    def work_send(zo):
        work(zo)
        rzc(lax.rem(zo + 1, no)).start()
    loop(0, no - 1, work_send)
    work(no - 1)

    def add_z(d, acc):
        rz_in(d).wait_recv()
        return acc + rz[zof(d)].astype(F32)
    total = lax.fori_loop(1, no, add_z, bsum[z].astype(F32))
    gram = jnp.zeros((k, k), F32)
    for b in range(nb):
        x = inv[b:b + 1] * (total[b] + fwd[b * k:(b + 1) * k] + own[b])
        img_ref[b] = x
        gram = gram + lax.dot_general(x, x, NT, preferred_element_type=F32, precision=HI)
    half = k // 2
    ginner[i] = jnp.concatenate([gram[:half], gram[half:]], axis=1)

    def g1(d):
        return remote(ginner.at[i], ginner.at[i], g1_s.at[d], g1_r.at[i], z, iof(d))

    def g1_in(d):
        ii = iof(d)
        return remote(ginner.at[ii], ginner.at[ii], g1_s.at[d], g1_r.at[ii], z, ii)

    def g2(d):
        return remote(gz.at[z], gz.at[z], g2_s.at[d], g2_r.at[z], zof(d), i)

    def g2_in(d):
        zz = zof(d)
        return remote(gz.at[zz], gz.at[zz], g2_s.at[d], g2_r.at[zz], zz, i)

    loop(1, ni, lambda d: g1(d).start())
    loop(1, ni, lambda d: g1_in(d).wait_recv())
    gz[z] = lax.fori_loop(1, ni, lambda j, a: a + ginner[j], ginner[0])
    loop(1, no, lambda d: g2(d).start())
    loop(1, no, lambda d: g2_in(d).wait_recv())
    g = lax.fori_loop(1, no, lambda j, a: a + gz[j], gz[0])
    gram_ref[...] = g * (1.0 / (n * nb * ts))

    loop(1, no, lambda d: vz(d).wait_send())
    loop(0, no, lambda zd: loop(1, nc, lambda d: vp(zd, d).wait_send()))
    loop(0, no, lambda zd: loop(0, nc, lambda d: vc(zd, d).wait_send()))
    loop(1, n, lambda d: cs(d).wait_send())
    loop(1, n, lambda d: iv(d).wait_send())
    loop(0, no, lambda zd: rc(zd).wait_send())
    loop(0, no, lambda zd: loop(1, nc, lambda d: rp(zd, d).wait_send()))
    loop(1, no, lambda zd: rzc(zd).wait_send())
    loop(1, ni, lambda d: g1(d).wait_send())
    loop(1, no, lambda d: g2(d).wait_send())


def orthonormalize(k, gram_ref, img_ref, deg_ref, out_ref, deg_out):
    deg_out[...] = deg_ref[...]
    g = gram_ref[...]
    a = jnp.concatenate([g[:, :k], g[:, k:]], axis=0)
    row = lax.broadcasted_iota(jnp.int32, (k, k), 0)
    col = lax.broadcasted_iota(jnp.int32, (k, k), 1)
    a = jnp.concatenate([a, jnp.where(row == col, 1.0, 0.0)], axis=1)
    rows = lax.broadcasted_iota(jnp.int32, (k, 2 * k), 0)
    scale = jnp.zeros((k, 2 * k), F32)
    for j0 in range(0, k, 8):
        cols = [jnp.broadcast_to(a[:, j0 + q:j0 + q + 1], (k, 2 * k)) for q in range(8)]
        lines = [a[j0 + q:j0 + q + 1] for q in range(8)]
        for q in range(8):
            c, j = cols[q], j0 + q
            over = 1.0 / c[j:j + 1]
            line = lines[q] * over
            scale = jnp.where(rows == j, c, scale)
            for p in range(q + 1, 8):
                at = c[j0 + p:j0 + p + 1]
                lines[p] = lines[p] - at * line
                cols[p] = cols[p] - c * (at * over)
            a = a - jnp.where(rows > j, c, 0.0) * line
    inv_low = (a * lax.rsqrt(scale))[:, k:]
    for b in range(img_ref.shape[0]):
        ts = img_ref.shape[2]
        out_ref[:, b * ts:(b + 1) * ts] = jnp.dot(
            inv_low, img_ref[b], preferred_element_type=F32, precision=HI)


def shards(tiles, tile_row, tile_col, counts, vectors):
    no, ni = lax.axis_size("outer"), lax.axis_size("inner")
    n = no * ni
    nc = ni // 2
    ns = tiles.shape[0] // n
    ts = tiles.shape[1]
    k = vectors.shape[1]
    nb = vectors.shape[0] // ts
    dma = pltpu.SemaphoreType.DMA
    blk = (nb, k, ts)
    vmem = pl.BlockSpec(memory_space=pltpu.VMEM)
    smem = pl.BlockSpec(memory_space=pltpu.SMEM)
    img, deg, gram = pl.pallas_call(
        functools.partial(exchange, no, ni, ns, nb, k, ts),
        out_shape=(
            jax.ShapeDtypeStruct(blk, F32),
            jax.ShapeDtypeStruct((nb, ts), F32),
            jax.ShapeDtypeStruct((k // 2, 2 * k), F32),
        ),
        in_specs=[smem, smem, smem, pl.BlockSpec(memory_space=pl.ANY), vmem],
        out_specs=(vmem, vmem, vmem),
        scratch_shapes=[
            pltpu.VMEM((n, ns * ts, ts), BF),
            pltpu.VMEM((n,) + blk, BF),
            pltpu.VMEM((n, nb, ts), F32),
            pltpu.VMEM((n, nb, ts), F32),
            pltpu.VMEM((n, nb, ts), F32),
            pltpu.VMEM(blk, F32),
            pltpu.VMEM((2, no, nc) + blk, BF),
            pltpu.VMEM((no, nc) + blk, BF),
            pltpu.VMEM((no, nc) + blk, BF),
            pltpu.VMEM((no, nc) + blk, BF),
            pltpu.VMEM((no,) + blk, BF),
            pltpu.VMEM((no,) + blk, BF),
            pltpu.VMEM((nb * k, ts), F32),
            pltpu.VMEM((ni, k // 2, 2 * k), F32),
            pltpu.VMEM((no, k // 2, 2 * k), F32),
            dma((no,)),
            dma((no,)), dma((no,)),
            dma((no, nc)), dma((no, nc)),
            dma((no, nc)), dma((no, nc)),
            dma((n,)), dma((n,)),
            dma((n,)), dma((n,)),
            dma((no,)), dma((no,)),
            dma((no, nc)), dma((no, nc)),
            dma((no,)), dma((no,)),
            dma((ni,)), dma((ni,)),
            dma((no,)), dma((no,)),
        ],
        compiler_params=pltpu.CompilerParams(
            collective_id=0, has_side_effects=True, vmem_limit_bytes=60 * 2**20),
        name="exchange",
    )(tile_row, tile_col, counts, tiles.reshape(n, ns * ts, ts), vectors.T)
    basis, deg = pl.pallas_call(
        functools.partial(orthonormalize, k),
        out_shape=(
            jax.ShapeDtypeStruct((k, nb * ts), F32),
            jax.ShapeDtypeStruct((nb, ts), F32),
        ),
        in_specs=[vmem, vmem, vmem],
        out_specs=(vmem, vmem),
        name="orthonormalize",
    )(gram, img, deg)
    return (basis.T, deg.reshape(nb * ts))


def solution(mesh):
    placed = (
        P(("outer", "inner"), None, None),
        P(("outer", "inner")),
        P(("outer", "inner")),
        P(("outer", "inner")),
        P(("outer", "inner"), None),
    )
    return jax.shard_map(
        shards,
        mesh=mesh,
        in_specs=placed,
        out_specs=(P(("outer", "inner"), None), P(("outer", "inner"))),
        check_vma=False,
    )
```

```python
import functools

import jax
import jax.numpy as jnp
from jax import lax
from jax.experimental import pallas as pl
from jax.experimental.pallas import tpu as pltpu
from jax.sharding import PartitionSpec as P

MESH = pl.DeviceIdType.MESH
BF = jnp.bfloat16
F32 = jnp.float32
NT = (((1,), (1,)), ((), ()))
HI = lax.Precision.HIGHEST


def exchange(
    no, ni, ns, nb, k, ts,
    row_ref, col_ref, cnt_ref, tiles_hbm, v_ref,
    img_ref, deg_ref, gram_ref,
    tiles, vall, csum, crecv, invall, own, mout, rcore, asum, rplane, bsum, rz, fwd, ginner, gz,
    tile_sem, vz_s, vz_r, vp_s, vp_r, vc_s, vc_r, cs_s, cs_r, iv_s, iv_r,
    rc_s, rc_r, rp_s, rp_r, rz_s, rz_r, g1_s, g1_r, g2_s, g2_r,
):
    nc = ni // 2
    n = no * ni
    z = lax.axis_index("outer")
    i = lax.axis_index("inner")
    me = z * ni + i
    chip = i // 2
    core = i % 2
    sib = chip * 2 + (1 - core)

    def zof(d):
        return lax.rem(z + d, no)

    def cof(d):
        return lax.rem(chip + d, nc)

    def iof(d):
        return lax.rem(i + d, ni)

    def hof(d):
        return lax.rem(me + d, n)

    def loop(lo, hi, body):
        def step(j, carry):
            body(j)
            return carry
        lax.fori_loop(lo, hi, step, 0)

    def remote(src, dst, ssem, rsem, zz, ii):
        return pltpu.make_async_remote_copy(
            src_ref=src, dst_ref=dst, send_sem=ssem, recv_sem=rsem,
            device_id=(zz, ii), device_id_type=MESH)

    def tile_copy(q):
        part = pl.ds(q * ni, ni)
        return pltpu.make_async_copy(tiles_hbm.at[part], tiles.at[part], tile_sem.at[q])

    for q in range(no):
        tile_copy(q).start()

    barrier = pltpu.get_barrier_semaphore()

    def greet(d):
        h = hof(d)
        pl.semaphore_signal(barrier, inc=1, device_id=(h // ni, h % ni), device_id_type=MESH)
    loop(1, n, greet)
    pl.semaphore_wait(barrier, n - 1)

    def vz(d):
        return remote(vall.at[me], vall.at[me], vz_s.at[d], vz_r.at[z], zof(d), i)

    def vz_in(d):
        zz = zof(d)
        return remote(vall.at[me], vall.at[zz * ni + i], vz_s.at[d], vz_r.at[zz], zz, i)

    def vp(zd, d):
        zz = zof(zd)
        slot = vall.at[zz * ni + i]
        return remote(slot, slot, vp_s.at[zd, d], vp_r.at[zz, chip], z, cof(d) * 2 + core)

    def vp_in(zd, d):
        zz, cc = zof(zd), cof(d)
        slot = vall.at[zz * ni + cc * 2 + core]
        return remote(slot, slot, vp_s.at[zd, d], vp_r.at[zz, cc], z, cc * 2 + core)

    def vc(zd, d):
        zz, cc = zof(zd), cof(d)
        slot = vall.at[zz * ni + cc * 2 + core]
        return remote(slot, slot, vc_s.at[zd, d], vc_r.at[zz, cc], z, sib)

    def vc_in(zd, d):
        zz, cc = zof(zd), cof(d)
        slot = vall.at[zz * ni + cc * 2 + (1 - core)]
        return remote(slot, slot, vc_s.at[zd, d], vc_r.at[zz, cc], z, sib)

    for b in range(nb):
        vall[me, b] = v_ref[:, b * ts:(b + 1) * ts]
    loop(1, no, lambda d: vz(d).start())
    loop(1, nc, lambda d: vp(0, d).start())
    vc(0, 0).start()

    iota8 = lax.broadcasted_iota(jnp.int32, (8, ts), 0)

    def live_index(ref, h, s):
        return jnp.where(s < cnt_ref[h], ref[h * ns + s], -1)

    def sums(h, racc):
        t = tiles[h]
        wc = jnp.concatenate(
            [jnp.where(iota8 == live_index(col_ref, h, s), 1.0, 0.0).astype(BF) for s in range(ns)], axis=1)
        csum[h] = jnp.dot(wc, t, preferred_element_type=F32)[:nb]
        for s in range(ns):
            wr = jnp.where(iota8 == live_index(row_ref, h, s), 1.0, 0.0).astype(BF)
            racc = racc + lax.dot_general(wr, t[s * ts:(s + 1) * ts], NT, preferred_element_type=F32)
        return racc

    racc = jnp.zeros((8, ts), F32)
    for q in range(no):
        tile_copy(q).wait()
        racc = lax.fori_loop(q * ni, (q + 1) * ni, sums, racc)

    def cs(d):
        h = hof(d)
        return remote(csum.at[h], crecv.at[me], cs_s.at[d], cs_r.at[me], h // ni, h % ni)

    def cs_in(d):
        h = hof(d)
        return remote(csum.at[h], crecv.at[h], cs_s.at[d], cs_r.at[h], h // ni, h % ni)

    loop(1, n, lambda d: cs(d).start())

    def relay_z(zd):
        vz_in(zd).wait_recv()
        loop(1, nc, lambda d: vp(zd, d).start())
        vc(zd, 0).start()
    loop(1, no, relay_z)

    def add_sums(d, acc):
        cs_in(d).wait_recv()
        return acc + crecv[hof(d)]
    degree = lax.fori_loop(1, n, add_sums, 1.0 + racc[:nb] + csum[me])
    deg_ref[...] = degree
    invall[me] = lax.rsqrt(degree)

    def iv(d):
        h = hof(d)
        return remote(invall.at[me], invall.at[me], iv_s.at[d], iv_r.at[me], h // ni, h % ni)

    def iv_in(d):
        h = hof(d)
        return remote(invall.at[h], invall.at[h], iv_s.at[d], iv_r.at[h], h // ni, h % ni)

    loop(1, n, lambda d: iv(d).start())

    inv = invall[me]
    for b in range(nb):
        own[b] = (inv[b:b + 1] * vall[me, b].astype(F32)).astype(BF).astype(F32)

    def mirror(zz, cc, half):
        h = zz * ni + cc * 2 + half
        parts = [[] for _ in range(nb)]
        for s in range(ns):
            c = live_index(col_ref, h, s)
            rows = own[row_ref[h * ns + s]]
            for b in range(nb):
                parts[b].append((rows * jnp.where(c == b, 1.0, 0.0)).astype(BF))
        left = jnp.concatenate([jnp.concatenate(p, axis=1) for p in parts], axis=0)
        m = jnp.dot(left, tiles[h], preferred_element_type=F32)
        mout[half, zz, cc] = m.astype(BF).reshape(nb, k, ts)

    def rc(zd):
        zz = zof(zd)
        return remote(mout.at[1 - core, zz], rcore.at[zz], rc_s.at[zz], rc_r.at[zz], z, sib)

    def rp(zd, d):
        zz, cc = zof(zd), cof(d)
        return remote(asum.at[zz, cc], rplane.at[zz, chip], rp_s.at[zd, d], rp_r.at[zz, chip], z, cc * 2 + core)

    def rp_in(zd, d):
        zz, cc = zof(zd), cof(d)
        return remote(asum.at[zz, cc], rplane.at[zz, cc], rp_s.at[zd, d], rp_r.at[zz, cc], z, cc * 2 + core)

    def rzc(zd):
        return remote(bsum.at[zof(zd)], rz.at[z], rz_s.at[zd], rz_r.at[z], zof(zd), i)

    def rz_in(zd):
        zz = zof(zd)
        return remote(bsum.at[zz], rz.at[zz], rz_s.at[zd], rz_r.at[zz], zz, i)

    def make_chunk(zo):
        zd = lax.rem(zo + 1, no)
        zz = zof(zd)
        loop(0, nc, lambda cc: mirror(zz, cc, 1 - core))
        rc(zd).start()
        loop(0, nc, lambda cc: mirror(zz, cc, core))

    def send_chunk(zo):
        zd = lax.rem(zo + 1, no)
        zz = zof(zd)
        rc(zd).wait_recv()

        def add_one(d):
            cc = cof(d)
            asum[zz, cc] = (mout[core, zz, cc].astype(F32) + rcore[zz, cc].astype(F32)).astype(BF)

        def add_send(d):
            add_one(d)
            rp(zd, d).start()
        loop(1, nc, add_send)
        add_one(0)
    make_chunk(0)

    def make_send(zo):
        make_chunk(zo)
        send_chunk(zo - 1)
    loop(1, no, make_send)
    send_chunk(no - 1)

    def relay_p(zd):
        def one(d):
            vp_in(zd, d).wait_recv()
            vc(zd, d).start()
        loop(1, nc, one)
    loop(0, no, relay_p)
    loop(1, n, lambda d: iv_in(d).wait_recv())
    loop(0, no, lambda zd: loop(0, nc, lambda d: vc_in(zd, d).wait_recv()))

    fwd[...] = jnp.zeros_like(fwd)

    def forward(h):
        acc = fwd[...]
        for s in range(ns):
            c = col_ref[h * ns + s]
            r = live_index(row_ref, h, s)
            blk = (inv_row(h, c) * vall[h, c].astype(F32)).astype(BF).astype(F32)
            left = jnp.concatenate([(blk * jnp.where(r == b, 1.0, 0.0)).astype(BF) for b in range(nb)], axis=0)
            acc = acc + lax.dot_general(left, tiles[h, s * ts:(s + 1) * ts], NT, preferred_element_type=F32)
        fwd[...] = acc

    def inv_row(h, c):
        rows = invall[h]
        out = rows[0:1]
        for b in range(1, nb):
            out = jnp.where(jnp.broadcast_to(c, out.shape) == b, rows[b:b + 1], out)
        return out

    def work(zo):
        zd = lax.rem(zo + 1, no)
        zz = zof(zd)
        total = asum[zz, chip].astype(F32)

        def add_p(d, acc):
            rp_in(zd, d).wait_recv()
            return acc + rplane[zz, cof(d)].astype(F32)
        total = lax.fori_loop(1, nc, add_p, total)
        bsum[zz] = total.astype(BF)

    def forward_chunk(zo):
        zz = zof(lax.rem(zo + 1, no))
        loop(zz * ni, (zz + 1) * ni, forward)

    def work_send(zo):
        work(zo)
        rzc(lax.rem(zo + 1, no)).start()
        forward_chunk(zo)
    loop(0, no - 1, work_send)
    work(no - 1)
    forward_chunk(no - 1)

    def add_z(d, acc):
        rz_in(d).wait_recv()
        return acc + rz[zof(d)].astype(F32)
    total = lax.fori_loop(1, no, add_z, bsum[z].astype(F32))
    gram = jnp.zeros((k, k), F32)
    for b in range(nb):
        x = inv[b:b + 1] * (total[b] + fwd[b * k:(b + 1) * k] + own[b])
        img_ref[b] = x
        gram = gram + lax.dot_general(x, x, NT, preferred_element_type=F32, precision=HI)
    half = k // 2
    ginner[i] = jnp.concatenate([gram[:half], gram[half:]], axis=1)

    def g1(d):
        return remote(ginner.at[i], ginner.at[i], g1_s.at[d], g1_r.at[i], z, iof(d))

    def g1_in(d):
        ii = iof(d)
        return remote(ginner.at[ii], ginner.at[ii], g1_s.at[d], g1_r.at[ii], z, ii)

    def g2(d):
        return remote(gz.at[z], gz.at[z], g2_s.at[d], g2_r.at[z], zof(d), i)

    def g2_in(d):
        zz = zof(d)
        return remote(gz.at[zz], gz.at[zz], g2_s.at[d], g2_r.at[zz], zz, i)

    loop(1, ni, lambda d: g1(d).start())
    loop(1, ni, lambda d: g1_in(d).wait_recv())
    gz[z] = lax.fori_loop(1, ni, lambda j, a: a + ginner[j], ginner[0])
    loop(1, no, lambda d: g2(d).start())
    loop(1, no, lambda d: g2_in(d).wait_recv())
    g = lax.fori_loop(1, no, lambda j, a: a + gz[j], gz[0])
    gram_ref[...] = g * (1.0 / (n * nb * ts))

    loop(1, no, lambda d: vz(d).wait_send())
    loop(0, no, lambda zd: loop(1, nc, lambda d: vp(zd, d).wait_send()))
    loop(0, no, lambda zd: loop(0, nc, lambda d: vc(zd, d).wait_send()))
    loop(1, n, lambda d: cs(d).wait_send())
    loop(1, n, lambda d: iv(d).wait_send())
    loop(0, no, lambda zd: rc(zd).wait_send())
    loop(0, no, lambda zd: loop(1, nc, lambda d: rp(zd, d).wait_send()))
    loop(1, no, lambda zd: rzc(zd).wait_send())
    loop(1, ni, lambda d: g1(d).wait_send())
    loop(1, no, lambda d: g2(d).wait_send())


def orthonormalize(k, gram_ref, img_ref, deg_ref, out_ref, deg_out):
    deg_out[...] = deg_ref[...]
    g = gram_ref[...]
    a = jnp.concatenate([g[:, :k], g[:, k:]], axis=0)
    row = lax.broadcasted_iota(jnp.int32, (k, k), 0)
    col = lax.broadcasted_iota(jnp.int32, (k, k), 1)
    a = jnp.concatenate([a, jnp.where(row == col, 1.0, 0.0)], axis=1)
    rows = lax.broadcasted_iota(jnp.int32, (k, 2 * k), 0)
    scale = jnp.zeros((k, 2 * k), F32)
    for j0 in range(0, k, 16):
        cols = [jnp.broadcast_to(a[:, j0 + q:j0 + q + 1], (k, 2 * k)) for q in range(16)]
        lines = [a[j0 + q:j0 + q + 1] for q in range(16)]
        for q in range(16):
            c, j = cols[q], j0 + q
            over = 1.0 / c[j:j + 1]
            line = lines[q] * over
            scale = jnp.where(rows == j, c, scale)
            for p in range(q + 1, 16):
                at = c[j0 + p:j0 + p + 1]
                lines[p] = lines[p] - at * line
                cols[p] = cols[p] - c * (at * over)
            a = a - jnp.where(rows > j, c, 0.0) * line
    inv_low = (a * lax.rsqrt(scale))[:, k:]
    for b in range(img_ref.shape[0]):
        ts = img_ref.shape[2]
        out_ref[:, b * ts:(b + 1) * ts] = jnp.dot(
            inv_low, img_ref[b], preferred_element_type=F32, precision=HI)


def shards(tiles, tile_row, tile_col, counts, vectors):
    no, ni = lax.axis_size("outer"), lax.axis_size("inner")
    n = no * ni
    nc = ni // 2
    ns = tiles.shape[0] // n
    ts = tiles.shape[1]
    k = vectors.shape[1]
    nb = vectors.shape[0] // ts
    dma = pltpu.SemaphoreType.DMA
    blk = (nb, k, ts)
    vmem = pl.BlockSpec(memory_space=pltpu.VMEM)
    smem = pl.BlockSpec(memory_space=pltpu.SMEM)
    img, deg, gram = pl.pallas_call(
        functools.partial(exchange, no, ni, ns, nb, k, ts),
        out_shape=(
            jax.ShapeDtypeStruct(blk, F32),
            jax.ShapeDtypeStruct((nb, ts), F32),
            jax.ShapeDtypeStruct((k // 2, 2 * k), F32),
        ),
        in_specs=[smem, smem, smem, pl.BlockSpec(memory_space=pl.ANY), vmem],
        out_specs=(vmem, vmem, vmem),
        scratch_shapes=[
            pltpu.VMEM((n, ns * ts, ts), BF),
            pltpu.VMEM((n,) + blk, BF),
            pltpu.VMEM((n, nb, ts), F32),
            pltpu.VMEM((n, nb, ts), F32),
            pltpu.VMEM((n, nb, ts), F32),
            pltpu.VMEM(blk, F32),
            pltpu.VMEM((2, no, nc) + blk, BF),
            pltpu.VMEM((no, nc) + blk, BF),
            pltpu.VMEM((no, nc) + blk, BF),
            pltpu.VMEM((no, nc) + blk, BF),
            pltpu.VMEM((no,) + blk, BF),
            pltpu.VMEM((no,) + blk, BF),
            pltpu.VMEM((nb * k, ts), F32),
            pltpu.VMEM((ni, k // 2, 2 * k), F32),
            pltpu.VMEM((no, k // 2, 2 * k), F32),
            dma((no,)),
            dma((no,)), dma((no,)),
            dma((no, nc)), dma((no, nc)),
            dma((no, nc)), dma((no, nc)),
            dma((n,)), dma((n,)),
            dma((n,)), dma((n,)),
            dma((no,)), dma((no,)),
            dma((no, nc)), dma((no, nc)),
            dma((no,)), dma((no,)),
            dma((ni,)), dma((ni,)),
            dma((no,)), dma((no,)),
        ],
        compiler_params=pltpu.CompilerParams(
            collective_id=0, has_side_effects=True, vmem_limit_bytes=60 * 2**20),
        name="exchange",
    )(tile_row, tile_col, counts, tiles.reshape(n, ns * ts, ts), vectors.T)
    basis, deg = pl.pallas_call(
        functools.partial(orthonormalize, k),
        out_shape=(
            jax.ShapeDtypeStruct((k, nb * ts), F32),
            jax.ShapeDtypeStruct((nb, ts), F32),
        ),
        in_specs=[vmem, vmem, vmem],
        out_specs=(vmem, vmem),
        name="orthonormalize",
    )(gram, img, deg)
    return (basis.T, deg.reshape(nb * ts))


def solution(mesh):
    placed = (
        P(("outer", "inner"), None, None),
        P(("outer", "inner")),
        P(("outer", "inner")),
        P(("outer", "inner")),
        P(("outer", "inner"), None),
    )
    return jax.shard_map(
        shards,
        mesh=mesh,
        in_specs=placed,
        out_specs=(P(("outer", "inner"), None), P(("outer", "inner"))),
        check_vma=False,
    )
```
